512 devices in a mesh: pages: 16 (over z, core), expert: 32 (over y, x).
Axes of the slice: x: 4, y: 8, z: 8, core: 2. Of those that a mesh axis runs over, the one named last changes fastest.
Arguments:
- queries: bfloat16 [247808, 576], P(('pages', 'expert')), may hold values from -6 to 6
- keys: bfloat16 [247808, 576], P(('pages', 'expert')), may hold values from -6 to 6
- values: bfloat16 [247808, 576], P(('pages', 'expert')), may hold values from -6 to 6
- resid: bfloat16 [247808, 576], P(('pages', 'expert')), may hold values from -6 to 6
- w_out: bfloat16 [576, 576], replicated, may hold values from -0.25 to 0.25
- w_merge: bfloat16 [2304, 1280], P(None, 'expert'), may hold values from -0.125 to 0.125
- rms_gain: float32 [1280], replicated, may hold values from 0.25 to 1.75
- w_gate: bfloat16 [32, 1280, 704], P('expert', 'pages'), may hold values from -0.15625 to 0.15625
- w_up: bfloat16 [32, 1280, 704], P('expert', 'pages'), may hold values from -0.15625 to 0.15625
- w_down: bfloat16 [32, 704, 1280], P('expert', None, 'pages'), may hold values from -0.21875 to 0.21875
- tile_count: int32 [16, 8], P('pages'), may hold values from 1 to 4, 20 in all within a row
- routes: int32 [61952, 6], P(('pages', 'expert')), may hold values from 0 to 31, all different within a row; in each aligned block of 121 rows (0 to 120, 121 to 241, ...) at most 30 rows name the same one
- route_weight: float32 [61952, 6], P(('pages', 'expert')), may hold values from 0.2 to 1
Outputs:
- layer_out: bfloat16 [61952, 1280], P(('pages', 'expert'))
The draws below stay inside these ranges and needn't reach their ends.
Inputs may be any that keep to these rules, and one draw needn't show every extreme that they name: `tile_count`: each page has 1 to 4 tiles; a group's counts sum to 20. `routes`: A token names 6 different experts; within the 121 rows of one tile no expert is named more than 30 times, and in some tile's rows one expert is named exactly 30 times.
All inputs are finite; a program needn't handle non-finite values.
Results may differ from the reference program's by a relative error of at most 0.014.
Values may be sent and summed in bfloat16 or wider, within the bound.
No kernel may reach another device: no remote copies, remote signals or barrier semaphores. Data moves between devices by JAX's collectives and lax.ppermute only.
A program may use at most 128 MiB of HBM per device.

```python
import math
import jax
import jax.numpy as jnp
import numpy as np
from jax import lax

HEADS = 8
HEAD_DIM = 72
VW = 576
TS = 22
D = 1280
H = 704
EXPERTS = 32
TOPK = 6
CAP = 30
MAXT = 4
ATT = 576
PATCH_DEV = 484
TOK_DEV = 121
MW = 2304
PAGE_G = 8
PATCHES = 247808
TOKENS = 61952
N_PAGES = 16
N_EXPERT = 32


def attention_pair(key):
    base = jax.random.fold_in(key, 4099)
    key_q, key_k = jax.random.split(base, 2)
    query_draw = jnp.clip(jax.random.normal(key_q, (PATCHES, ATT), jnp.float32), -6.0, 6.0)
    key_draw = jnp.clip(jax.random.normal(key_k, (PATCHES, ATT), jnp.float32), -6.0, 6.0)
    return (query_draw, key_draw)


def draw_queries(key, part):
    return attention_pair(key)[0].astype(jnp.bfloat16)


def draw_keys(key, part):
    return attention_pair(key)[1].astype(jnp.bfloat16)


def level_of(rng, extent, pieces, least, top_value):
    def one(dim, parts):
        steps = jax.random.uniform(jax.random.fold_in(jax.random.fold_in(rng, 6), dim), (parts,), jnp.float32, least / len(pieces), top_value / len(pieces))
        return jnp.repeat(jnp.exp(steps), extent[dim] // parts).reshape((-1,) + (1,) * (len(extent) - dim - 1))

    loudness = one(*pieces[0])
    for cut in pieces[1:]:
        loudness = loudness * one(*cut)
    return loudness


def profile(count, total, most, skew):
    portions = [(1 << 20) // math.isqrt(rank ** skew) + 1 for rank in range(2, count + 1)]
    rest, counts = total - most - (count - 1), [1] * (count - 1)
    while rest > 0:
        movable = [i for i in range(count - 1) if counts[i] < most]
        pool, budget = sum([portions[i] for i in movable]), rest
        for i in movable:
            more = min(most - counts[i], max(1, budget * portions[i] // pool), rest)
            counts[i] = counts[i] + more
            rest = rest - more
    return np.array([most] + counts)


def uneven_parts(rng, amount, total, reach, slope):
    if amount == 2:
        one = jax.random.randint(rng, (), max(1, total - reach), min(reach, total - 1) + 1)
        return jnp.stack([one, total - one])
    lengths = jnp.asarray(profile(amount, total, reach, slope), jnp.int32)
    pairs = (amount - 1) // 2
    source_of, taker = lengths[1:1 + 2 * pairs:2], lengths[2:2 + 2 * pairs:2]
    room = jnp.minimum(source_of - 1, reach - taker)
    moved = jax.random.randint(jax.random.fold_in(rng, 1), (pairs,), 0, 1 << 20) % (room + 1)
    lengths = lengths.at[1:1 + 2 * pairs:2].set(source_of - moved).at[2:2 + 2 * pairs:2].set(taker + moved)
    return lengths[jax.random.permutation(jax.random.fold_in(rng, 2), amount)]


def deal_out(key, own, number, rows, amount, top, reach, skew):
    order = jax.random.permutation(key, amount)
    packed, ordinary = portions_of(amount, rows * top, reach, skew, True), portions_of(amount, rows * top, reach, skew, False)
    places = jnp.arange(amount)

    def named(lengths, turn):
        used = int((lengths > 0).sum())
        fixed = max(1, used // 4)
        shifted = fixed + (places - fixed + turn * (used - fixed)) % max(1, amount - fixed)
        return jnp.zeros((amount,), jnp.int32).at[order[jnp.where(places < fixed, places, shifted)]].set(jnp.asarray(lengths, jnp.int32))

    lengths = jnp.where(number % 4 == 0, named(packed, number // 4), named(ordinary, number - number // 4 - 1))
    mixed = jax.random.permutation(jax.random.fold_in(own, 3), amount)
    donor, receiver = mixed[0:amount // 2 * 2:2], mixed[1:amount // 2 * 2:2]
    slack = jnp.minimum(lengths[donor] - 1, reach - lengths[receiver]) // 2
    slack = jnp.where((donor == order[0]) | (receiver == order[0]) | (lengths[receiver] == 0), 0, jnp.maximum(slack, 0))
    shifted = jax.random.randint(jax.random.fold_in(own, 4), (amount // 2,), 0, 1 << 20) % (slack + 1)
    lengths = lengths.at[donor].add(-shifted).at[receiver].add(shifted)
    members = jnp.searchsorted(jnp.cumsum(lengths), jnp.arange(rows * top), side="right").astype(jnp.int32)
    listing = members.reshape(top, rows).T
    listing = listing[jax.random.permutation(jax.random.fold_in(own, 1), rows)]
    turn = jax.random.randint(jax.random.fold_in(own, 2), (rows, 1), 0, top)
    return jnp.take_along_axis(listing, (jnp.arange(top)[None, :] + turn) % top, axis=1)


def portions_of(count, total, reach, slope, full):
    portions = [(1 << 20) // math.isqrt(rank ** slope) + 1 for rank in range(1, count + 1)]
    largest = reach if full else min(reach, max(-(-total // count), total * portions[0] // sum(portions)))
    least = 1 if total - largest >= count - 1 else 0
    counts, surplus = [largest] + [least] * (count - 1), total - largest - least * (count - 1)
    while surplus > 0:
        free = [i for i in range(1, count) if counts[i] < largest] or [i for i in range(1, count) if counts[i] < reach]
        pool, remaining = sum([portions[i] for i in free]), surplus
        for i in free:
            addition = min(reach - counts[i], max(1, remaining * portions[i] // pool), surplus)
            counts[i] = counts[i] + addition
            surplus = surplus - addition
    return np.array(counts)


def scatter_about(rng, shape, width, reach, pieces=(), kind=jnp.bfloat16):
    values = jax.random.normal(rng, shape, jnp.float32) * width
    if len(pieces) > 0:
        values = level_of(rng, shape, pieces, -0.22, 0.18) * values
    return jnp.clip(values, min=-reach, max=reach).astype(kind)


def setup_inputs(seed: int = 0) -> dict:
    splits = jax.random.split(jax.random.key(seed), 14)
    queries = draw_queries(jax.random.fold_in(splits[13], 71), 0)
    keys = draw_keys(jax.random.fold_in(splits[13], 71), 0)
    values = scatter_about(splits[2], (PATCHES, ATT), 1.0, 6.0, ((0, 512),))
    resid = scatter_about(splits[3], (PATCHES, VW), 1.0, 6.0, ((0, 512),))
    w_out = scatter_about(splits[4], (ATT, VW), ATT ** -0.5, 0.25)
    w_merge = scatter_about(splits[5], (MW, D), MW ** -0.5, 0.125, ((1, 32),))
    rms_gain = jnp.clip(1.0 + 0.15 * jax.random.normal(splits[6], (D,), jnp.float32), 0.25, 1.75)
    w_gate = scatter_about(splits[7], (EXPERTS, D, H), D ** -0.5, 0.15625, ((0, 32), (1, 16)))
    w_up = scatter_about(splits[8], (EXPERTS, D, H), D ** -0.5, 0.15625, ((0, 32), (1, 16)))
    w_down = scatter_about(splits[9], (EXPERTS, H, D), H ** -0.5, 0.21875, ((0, 32), (2, 16)))
    tile_count = jax.vmap(lambda own: uneven_parts(own, PAGE_G, PAGE_G * 5 // 2, MAXT, 0))(jax.random.split(splits[10], N_PAGES)).reshape((N_PAGES, PAGE_G)).astype(jnp.int32)
    routes_keys = jax.random.split(jax.random.fold_in(splits[11], 1), TOKENS // TOK_DEV)
    routes_turns = jax.random.permutation(jax.random.fold_in(splits[11], 3), TOKENS // TOK_DEV)
    routes = jax.vmap(lambda own, number: deal_out(jax.random.fold_in(splits[11], 2), own, number, TOK_DEV, EXPERTS, TOPK, CAP, 2))(routes_keys, routes_turns).reshape((TOKENS, TOPK))
    route_weight = jnp.clip(0.2 + 0.8 * jax.random.uniform(splits[12], (TOKENS, TOPK), jnp.float32) ** level_of(splits[12], (TOKENS, TOPK), ((0, 512),), -0.2, 0.2), 0.2, 1.0)
    return dict(queries=queries, keys=keys, values=values, resid=resid, w_out=w_out, w_merge=w_merge, rms_gain=rms_gain, w_gate=w_gate, w_up=w_up, w_down=w_down, tile_count=tile_count, routes=routes, route_weight=route_weight)


def attention_tiles(queries, keys, values, resid, w_out):
    count = queries.shape[0]
    shaped = (count, PATCH_DEV, HEADS, HEAD_DIM)
    q_heads = queries.astype(jnp.float32).reshape(shaped)
    k_heads = keys.astype(jnp.float32).reshape(shaped)
    v_heads = values.astype(jnp.float32).reshape(shaped)
    scores = jnp.einsum('nqhd,nkhd->nhqk', q_heads, k_heads) * HEAD_DIM ** (-0.5)
    top = lax.optimization_barrier(jnp.max(scores, axis=-1, keepdims=True))
    weights = jnp.exp(scores - top)
    probs = (weights / lax.optimization_barrier(jnp.sum(weights, axis=-1, keepdims=True))).astype(jnp.bfloat16)
    probs = lax.optimization_barrier(probs).astype(jnp.float32)
    attended = jnp.einsum('nhqk,nkhd->nqhd', probs, v_heads).astype(jnp.bfloat16)
    attended = lax.optimization_barrier(attended).astype(jnp.float32).reshape(count, PATCH_DEV, ATT)
    update = jnp.einsum('nqa,ac->nqc', attended, w_out.astype(jnp.float32))
    return (resid.astype(jnp.float32) + update).astype(jnp.bfloat16)

def space_to_depth(vis):
    count = vis.shape[0]
    half = TS // 2
    grid = vis.reshape(count, half, 2, half, 2, VW).transpose(0, 1, 3, 2, 4, 5)
    return grid.reshape(count, half * half, 4 * VW)

def slot_targets(route_block):
    flat = route_block.reshape(-1)
    onehot = (flat[:, None] == jnp.arange(EXPERTS, dtype=jnp.int32)[None, :]).astype(jnp.int32)
    before = jnp.cumsum(onehot, axis=0) - onehot
    return (flat * CAP + lax.optimization_barrier(jnp.sum(before * onehot, axis=1))).astype(jnp.int32)

def dispatch_table(target):
    table = (jnp.arange(EXPERTS * CAP, dtype=jnp.int32)[:, None] == target[None, :]).astype(jnp.float32)
    return lax.optimization_barrier(jnp.sum(table.reshape(EXPERTS * CAP, TOK_DEV, TOPK), axis=2))

def pick_rows(rows, index):
    return rows[index]

def reference(queries, keys, values, resid, w_out, w_merge, rms_gain, w_gate, w_up, w_down, tile_count, routes, route_weight):
    position = jnp.arange(N_EXPERT, dtype=jnp.int32)
    live = (position % MAXT)[None, :] < tile_count[:, position // MAXT]
    gate_all = w_gate.astype(jnp.float32)
    up_all = w_up.astype(jnp.float32)
    down_all = w_down.astype(jnp.float32)

    def one_group(pack):
        q_part, k_part, v_part, r_part, alive, route_part, weight_part = pack
        vis = attention_tiles(q_part, k_part, v_part, r_part, w_out)
        merged = jnp.where(alive[:, None, None], space_to_depth(vis), jnp.zeros((), jnp.bfloat16)).astype(jnp.bfloat16)
        proj = jnp.dot(merged.reshape(N_EXPERT * TOK_DEV, MW), w_merge, preferred_element_type=jnp.float32)
        stream = jax.nn.gelu(proj, approximate=False).astype(jnp.bfloat16)
        wide = lax.optimization_barrier(stream).astype(jnp.float32)
        normed = (wide * lax.rsqrt(lax.optimization_barrier(jnp.mean(wide * wide, axis=-1, keepdims=True)) + 1e-06) * rms_gain).astype(jnp.bfloat16)
        blocks = lax.optimization_barrier(normed).astype(jnp.float32).reshape(N_EXPERT, TOK_DEV, D)
        targets = jax.vmap(slot_targets)(route_part)
        tables = jax.vmap(dispatch_table)(targets)
        send = jnp.einsum('nst,ntd->nsd', tables, blocks).astype(jnp.bfloat16)
        recv = send.reshape(N_EXPERT, EXPERTS, CAP, D).transpose(1, 0, 2, 3).reshape(EXPERTS, N_EXPERT * CAP, D)
        recv = lax.optimization_barrier(recv).astype(jnp.float32)
        gate = jnp.einsum('erd,edh->erh', recv, gate_all)
        up = jnp.einsum('erd,edh->erh', recv, up_all)
        act = (jax.nn.silu(gate) * up).astype(jnp.bfloat16)
        act = lax.optimization_barrier(act).astype(jnp.float32)
        outcome = jnp.einsum('erh,ehd->erd', act, down_all).astype(jnp.bfloat16)
        back = outcome.reshape(EXPERTS, N_EXPERT, CAP, D).transpose(1, 0, 2, 3).reshape(N_EXPERT, EXPERTS * CAP, D)
        picked = jax.vmap(pick_rows)(back, targets)
        picked = lax.optimization_barrier(picked).astype(jnp.float32).reshape(N_EXPERT, TOK_DEV, TOPK, D)
        total = wide.reshape(N_EXPERT, TOK_DEV, D) + lax.optimization_barrier(jnp.sum(weight_part[..., None] * picked, axis=2))
        return total.astype(jnp.bfloat16)
    grouped = (queries.reshape(N_PAGES, N_EXPERT, PATCH_DEV, ATT), keys.reshape(N_PAGES, N_EXPERT, PATCH_DEV, ATT), values.reshape(N_PAGES, N_EXPERT, PATCH_DEV, ATT), resid.reshape(N_PAGES, N_EXPERT, PATCH_DEV, VW), live, routes.reshape(N_PAGES, N_EXPERT, TOK_DEV, TOPK), route_weight.reshape(N_PAGES, N_EXPERT, TOK_DEV, TOPK))
    result = lax.map(one_group, grouped)
    return result.reshape(TOKENS, D)
```

```python
import functools
import jax
import jax.numpy as jnp
from jax import lax
from jax.experimental import pallas as pl
from jax.experimental.pallas import tpu as pltpu
from jax.sharding import Mesh
from jax.sharding import PartitionSpec as P

HEADS = 8
TS = 22
EXPERTS = 32
TOPK = 6
MAXT = 4
SLOT = 32
TPAD = 128


def tile_attention(queries, keys, values, resid, w_out):
    patches = queries.shape[0]
    head_size = queries.shape[1] // HEADS
    q_heads = queries.reshape(patches, HEADS, head_size)
    k_heads = keys.reshape(patches, HEADS, head_size)
    v_heads = values.reshape(patches, HEADS, head_size)
    scores = jnp.einsum(
        "qhd,khd->hqk", q_heads, k_heads, preferred_element_type=jnp.float32
    ) * head_size ** (-0.5)
    top = jnp.max(scores, axis=-1, keepdims=True)
    weights = jnp.exp(scores - top)
    probs = (weights / jnp.sum(weights, axis=-1, keepdims=True)).astype(jnp.bfloat16)
    attended = jnp.einsum(
        "hqk,khd->qhd", probs, v_heads, preferred_element_type=jnp.float32
    ).astype(jnp.bfloat16)
    update = jnp.dot(attended.reshape(patches, -1), w_out, preferred_element_type=jnp.float32)
    return (resid.astype(jnp.float32) + update).astype(jnp.bfloat16)


def space_to_depth(vis):
    half = TS // 2
    width = vis.shape[1]
    grid = vis.reshape(half, 2, half, 2, width).transpose(0, 2, 1, 3, 4)
    return grid.reshape(half * half, 4 * width)


def slot_tables(routes, route_weight):
    tokens = routes.shape[0]
    routes = jnp.pad(routes, ((0, TPAD - tokens), (0, 0)), constant_values=-1)
    route_weight = jnp.pad(route_weight, ((0, TPAD - tokens), (0, 0)))
    hit = routes.T[:, None, :] == jnp.arange(EXPERTS, dtype=jnp.int32)[None, :, None]
    member = jnp.any(hit, axis=0)
    weight = jnp.sum(jnp.where(hit, route_weight.T[:, None, :], 0.0), axis=0)
    earlier = jnp.triu(jnp.ones((TPAD, TPAD), jnp.bfloat16), 1)
    before = jnp.dot(
        member.astype(jnp.bfloat16), earlier, preferred_element_type=jnp.float32
    ).astype(jnp.int32)
    place = jnp.where(member, before, -1)
    table = place[:, None, :] == jnp.arange(SLOT, dtype=jnp.int32)[None, :, None]
    high = weight.astype(jnp.bfloat16)
    low = (weight - high.astype(jnp.float32)).astype(jnp.bfloat16)
    zero = jnp.zeros((), jnp.bfloat16)
    rows = EXPERTS * SLOT
    return (
        table.astype(jnp.bfloat16).reshape(rows, TPAD),
        jnp.where(table, high[:, None, :], zero).reshape(rows, TPAD),
        jnp.where(table, low[:, None, :], zero).reshape(rows, TPAD),
    )


def merge_body(merged_ref, weight_ref, table_ref, stream_ref, send_ref):
    half = weight_ref.shape[2]
    dims = (((1,), (1,)), ((), ()))
    product = lax.dot_general(
        merged_ref[:, :half], weight_ref[0], dims, preferred_element_type=jnp.float32
    ) + lax.dot_general(
        merged_ref[:, half:], weight_ref[1], dims, preferred_element_type=jnp.float32
    )
    gelu = 0.5 * product * (1.0 + lax.erf(product * (0.5**0.5)))
    stream = gelu.astype(jnp.bfloat16)
    stream_ref[...] = stream
    rows = jnp.dot(table_ref[...], stream, preferred_element_type=jnp.float32)
    send_ref[...] = rows.astype(jnp.bfloat16).reshape(send_ref.shape)


def merge_dispatch(merged, weight, table):
    width = weight.shape[1]
    block = 256
    return pl.pallas_call(
        merge_body,
        grid=(width // block,),
        in_specs=[
            pl.BlockSpec(merged.shape, lambda i: (0, 0)),
            pl.BlockSpec((2, block, weight.shape[2]), lambda i: (0, i, 0)),
            pl.BlockSpec(table.shape, lambda i: (0, 0)),
        ],
        out_specs=[
            pl.BlockSpec((TPAD, block), lambda i: (0, i)),
            pl.BlockSpec((EXPERTS, SLOT, block), lambda i: (0, 0, i)),
        ],
        out_shape=[
            jax.ShapeDtypeStruct((TPAD, width), jnp.bfloat16),
            jax.ShapeDtypeStruct((EXPERTS, SLOT, width), jnp.bfloat16),
        ],
        compiler_params=pltpu.CompilerParams(vmem_limit_bytes=40 << 20),
        cost_estimate=pl.CostEstimate(
            flops=2 * TPAD * width * (merged.shape[1] + EXPERTS * SLOT),
            bytes_accessed=10 << 20,
            transcendentals=TPAD * width,
        ),
        name="merge_dispatch",
    )(merged, weight, table)


def expert_body(hidden, rows_ref, gain_ref, weight_ref, out_ref):
    wide = rows_ref[...].astype(jnp.float32)
    scale = lax.rsqrt(jnp.mean(wide * wide, axis=-1, keepdims=True) + 1e-06)
    normed = (wide * scale * gain_ref[...]).astype(jnp.bfloat16)
    both = jnp.dot(normed, weight_ref[:, : 2 * hidden], preferred_element_type=jnp.float32)
    gate = both[:, :hidden]
    up = both[:, hidden:]
    act = (gate / (1.0 + jnp.exp(-gate)) * up).astype(jnp.bfloat16)
    out_ref[...] = lax.dot_general(
        act,
        weight_ref[:, 2 * hidden :],
        (((1,), (1,)), ((), ())),
        preferred_element_type=jnp.float32,
    ).astype(jnp.bfloat16)


def expert_ffn(rows, gain, weight):
    count, width = rows.shape
    hidden = weight.shape[1] // 3
    block = 256
    return pl.pallas_call(
        functools.partial(expert_body, hidden),
        grid=(count // block,),
        in_specs=[
            pl.BlockSpec((block, width), lambda i: (i, 0)),
            pl.BlockSpec((1, width), lambda i: (0, 0)),
            pl.BlockSpec(weight.shape, lambda i: (0, 0)),
        ],
        out_specs=pl.BlockSpec((block, width), lambda i: (i, 0)),
        out_shape=jax.ShapeDtypeStruct((count, width), jnp.bfloat16),
        compiler_params=pltpu.CompilerParams(vmem_limit_bytes=48 << 20),
        cost_estimate=pl.CostEstimate(
            flops=6 * count * width * hidden,
            bytes_accessed=11 << 20,
            transcendentals=count * hidden,
        ),
        name="expert_ffn",
    )(rows, gain, weight)


def combine_body(stream_ref, high_ref, low_ref, back_ref, out_ref):
    dims = (((0,), (0,)), ((), ()))
    back = back_ref[...]
    total = lax.dot_general(
        high_ref[...], back, dims, preferred_element_type=jnp.float32
    ) + lax.dot_general(low_ref[...], back, dims, preferred_element_type=jnp.float32)
    total = total + stream_ref[...].astype(jnp.float32)
    out_ref[...] = total[: out_ref.shape[0]].astype(jnp.bfloat16)


def combine(stream, high, low, back, tokens):
    width = stream.shape[1]
    block = 256
    whole = lambda i: (0, 0)
    column = lambda i: (0, i)
    return pl.pallas_call(
        combine_body,
        grid=(width // block,),
        in_specs=[
            pl.BlockSpec((TPAD, block), column),
            pl.BlockSpec(high.shape, whole),
            pl.BlockSpec(low.shape, whole),
            pl.BlockSpec((back.shape[0], block), column),
        ],
        out_specs=pl.BlockSpec((tokens, block), column),
        out_shape=jax.ShapeDtypeStruct((tokens, width), jnp.bfloat16),
        compiler_params=pltpu.CompilerParams(vmem_limit_bytes=40 << 20),
        cost_estimate=pl.CostEstimate(
            flops=4 * TPAD * width * back.shape[0],
            bytes_accessed=4 << 20,
            transcendentals=0,
        ),
        name="combine",
    )(stream, high, low, back)


def local(
    queries,
    keys,
    values,
    resid,
    w_out,
    w_merge,
    rms_gain,
    w_gate,
    w_up,
    w_down,
    tile_count,
    routes,
    route_weight,
):
    tokens = routes.shape[0]
    position = lax.axis_index("y") * lax.axis_size("x") + lax.axis_index("x")
    page = position // MAXT
    count = lax.dynamic_index_in_dim(tile_count[0], page, keepdims=False)
    live = position % MAXT < count

    half = w_merge.shape[0] // 2
    piece = lax.dynamic_slice_in_dim(w_merge.T, lax.axis_index("core") * half, half, 1)
    piece = lax.all_gather(piece, "x", axis=0, tiled=True)
    merger = lax.all_gather(piece, ("core", "y"), axis=0, tiled=True)
    merger = merger.reshape(2, -1, half)

    mine = jnp.concatenate([w_gate[0], w_up[0], w_down[0].T], axis=1)
    mine, merger = lax.optimization_barrier((mine, merger))
    experts = lax.all_gather(mine, ("z", "core"), axis=0, tiled=True)

    table, high, low = slot_tables(routes, route_weight)
    vis = tile_attention(queries, keys, values, resid, w_out)
    merged = jnp.where(live, space_to_depth(vis), jnp.zeros((), jnp.bfloat16))
    merged = jnp.pad(merged, ((0, TPAD - tokens), (0, 0)))
    stream, send = merge_dispatch(merged, merger, table)
    received = lax.all_to_all(send, ("y", "x"), split_axis=0, concat_axis=0)
    width = stream.shape[1]
    outcome = expert_ffn(received.reshape(-1, width), rms_gain[None, :], experts)
    back = lax.all_to_all(
        outcome.reshape(EXPERTS, SLOT, width), ("y", "x"), split_axis=0, concat_axis=0
    )
    return combine(stream, high, low, back.reshape(-1, width), tokens)


def solution(mesh):
    inner = Mesh(mesh.devices.reshape(8, 2, 8, 4), ("z", "core", "y", "x"))
    pages = ("z", "core")
    expert = ("y", "x")
    rows = P(("z", "core", "y", "x"), None)
    return jax.shard_map(
        local,
        mesh=inner,
        in_specs=(
            rows,
            rows,
            rows,
            rows,
            P(),
            P(None, expert),
            P(),
            P(expert, pages, None),
            P(expert, pages, None),
            P(expert, None, pages),
            P(pages, None),
            rows,
            rows,
        ),
        out_specs=rows,
        check_vma=False,
    )
```

```python
import functools
import jax
import jax.numpy as jnp
from jax import lax
from jax.experimental import pallas as pl
from jax.experimental.pallas import tpu as pltpu
from jax.sharding import Mesh
from jax.sharding import PartitionSpec as P

HEADS = 8
TS = 22
EXPERTS = 32
TOPK = 6
MAXT = 4
SLOT = 32
TPAD = 128


def tile_attention(queries, keys, values, resid, w_out):
    patches = queries.shape[0]
    head_size = queries.shape[1] // HEADS
    q_heads = queries.reshape(patches, HEADS, head_size)
    k_heads = keys.reshape(patches, HEADS, head_size)
    v_heads = values.reshape(patches, HEADS, head_size)
    scores = jnp.einsum(
        "qhd,khd->hqk", q_heads, k_heads, preferred_element_type=jnp.float32
    ) * head_size ** (-0.5)
    top = jnp.max(scores, axis=-1, keepdims=True)
    weights = jnp.exp(scores - top)
    probs = (weights / jnp.sum(weights, axis=-1, keepdims=True)).astype(jnp.bfloat16)
    attended = jnp.einsum(
        "hqk,khd->qhd", probs, v_heads, preferred_element_type=jnp.float32
    ).astype(jnp.bfloat16)
    update = jnp.dot(attended.reshape(patches, -1), w_out, preferred_element_type=jnp.float32)
    return (resid.astype(jnp.float32) + update).astype(jnp.bfloat16)


def space_to_depth(vis):
    half = TS // 2
    width = vis.shape[1]
    grid = vis.reshape(half, 2, half, 2, width).transpose(0, 2, 1, 3, 4)
    return grid.reshape(half * half, 4 * width)


def slot_tables(routes, route_weight):
    tokens = routes.shape[0]
    routes = jnp.pad(routes, ((0, TPAD - tokens), (0, 0)), constant_values=-1)
    route_weight = jnp.pad(route_weight, ((0, TPAD - tokens), (0, 0)))
    hit = routes.T[:, None, :] == jnp.arange(EXPERTS, dtype=jnp.int32)[None, :, None]
    member = jnp.any(hit, axis=0)
    weight = jnp.sum(jnp.where(hit, route_weight.T[:, None, :], 0.0), axis=0)
    earlier = jnp.triu(jnp.ones((TPAD, TPAD), jnp.bfloat16), 1)
    before = jnp.dot(
        member.astype(jnp.bfloat16), earlier, preferred_element_type=jnp.float32
    ).astype(jnp.int32)
    place = jnp.where(member, before, -1)
    table = place[:, None, :] == jnp.arange(SLOT, dtype=jnp.int32)[None, :, None]
    high = weight.astype(jnp.bfloat16)
    low = (weight - high.astype(jnp.float32)).astype(jnp.bfloat16)
    zero = jnp.zeros((), jnp.bfloat16)
    rows = EXPERTS * SLOT
    return (
        table.astype(jnp.bfloat16).reshape(rows, TPAD),
        jnp.where(table, high[:, None, :], zero).reshape(rows, TPAD),
        jnp.where(table, low[:, None, :], zero).reshape(rows, TPAD),
    )


def merge_body(merged_ref, weight_ref, table_ref, stream_ref, send_ref):
    half = weight_ref.shape[2]
    dims = (((1,), (1,)), ((), ()))
    product = lax.dot_general(
        merged_ref[:, :half], weight_ref[0], dims, preferred_element_type=jnp.float32
    ) + lax.dot_general(
        merged_ref[:, half:], weight_ref[1], dims, preferred_element_type=jnp.float32
    )
    gelu = 0.5 * product * (1.0 + lax.erf(product * (0.5**0.5)))
    stream = gelu.astype(jnp.bfloat16)
    stream_ref[...] = stream
    rows = jnp.dot(table_ref[...], stream, preferred_element_type=jnp.float32)
    send_ref[...] = rows.astype(jnp.bfloat16).reshape(send_ref.shape)


def merge_dispatch(merged, weight, table):
    width = weight.shape[1]
    block = 256
    return pl.pallas_call(
        merge_body,
        grid=(width // block,),
        in_specs=[
            pl.BlockSpec(merged.shape, lambda i: (0, 0)),
            pl.BlockSpec((2, block, weight.shape[2]), lambda i: (0, i, 0)),
            pl.BlockSpec(table.shape, lambda i: (0, 0)),
        ],
        out_specs=[
            pl.BlockSpec((TPAD, block), lambda i: (0, i)),
            pl.BlockSpec((EXPERTS, SLOT, block), lambda i: (0, 0, i)),
        ],
        out_shape=[
            jax.ShapeDtypeStruct((TPAD, width), jnp.bfloat16),
            jax.ShapeDtypeStruct((EXPERTS, SLOT, width), jnp.bfloat16),
        ],
        compiler_params=pltpu.CompilerParams(vmem_limit_bytes=60 << 20),
        cost_estimate=pl.CostEstimate(
            flops=2 * TPAD * width * (merged.shape[1] + EXPERTS * SLOT),
            bytes_accessed=10 << 20,
            transcendentals=TPAD * width,
        ),
        name="merge_dispatch",
    )(merged, weight, table)


def expert_body(hidden, rows_ref, gain_ref, weight_ref, out_ref):
    gain = gain_ref[...]
    part = rows_ref.shape[0] // 2
    for i in range(2):
        span = pl.ds(i * part, part)
        wide = rows_ref[span].astype(jnp.float32)
        scale = lax.rsqrt(jnp.mean(wide * wide, axis=-1, keepdims=True) + 1e-06)
        normed = (wide * scale * gain).astype(jnp.bfloat16)
        both = jnp.dot(normed, weight_ref[:, : 2 * hidden], preferred_element_type=jnp.float32)
        gate = both[:, :hidden]
        up = both[:, hidden:]
        act = (gate / (1.0 + jnp.exp(-gate)) * up).astype(jnp.bfloat16)
        out_ref[span] = lax.dot_general(
            act,
            weight_ref[:, 2 * hidden :],
            (((1,), (1,)), ((), ())),
            preferred_element_type=jnp.float32,
        ).astype(jnp.bfloat16)


def expert_ffn(rows, gain, weight):
    count, width = rows.shape
    hidden = weight.shape[1] // 3
    block = 256
    return pl.pallas_call(
        functools.partial(expert_body, hidden),
        grid=(count // block,),
        in_specs=[
            pl.BlockSpec((block, width), lambda i: (i, 0)),
            pl.BlockSpec((1, width), lambda i: (0, 0)),
            pl.BlockSpec(weight.shape, lambda i: (0, 0)),
        ],
        out_specs=pl.BlockSpec((block, width), lambda i: (i, 0)),
        out_shape=jax.ShapeDtypeStruct((count, width), jnp.bfloat16),
        compiler_params=pltpu.CompilerParams(vmem_limit_bytes=60 << 20),
        cost_estimate=pl.CostEstimate(
            flops=6 * count * width * hidden,
            bytes_accessed=11 << 20,
            transcendentals=count * hidden,
        ),
        name="expert_ffn",
    )(rows, gain, weight)


def combine_body(stream_ref, high_ref, low_ref, back_ref, out_ref):
    dims = (((0,), (0,)), ((), ()))
    back = back_ref[...]
    total = lax.dot_general(
        high_ref[...], back, dims, preferred_element_type=jnp.float32
    ) + lax.dot_general(low_ref[...], back, dims, preferred_element_type=jnp.float32)
    total = total + stream_ref[...].astype(jnp.float32)
    out_ref[...] = total[: out_ref.shape[0]].astype(jnp.bfloat16)


def combine(stream, high, low, back, tokens):
    width = stream.shape[1]
    block = 256
    whole = lambda i: (0, 0)
    column = lambda i: (0, i)
    return pl.pallas_call(
        combine_body,
        grid=(width // block,),
        in_specs=[
            pl.BlockSpec((TPAD, block), column),
            pl.BlockSpec(high.shape, whole),
            pl.BlockSpec(low.shape, whole),
            pl.BlockSpec((back.shape[0], block), column),
        ],
        out_specs=pl.BlockSpec((tokens, block), column),
        out_shape=jax.ShapeDtypeStruct((tokens, width), jnp.bfloat16),
        compiler_params=pltpu.CompilerParams(vmem_limit_bytes=60 << 20),
        cost_estimate=pl.CostEstimate(
            flops=4 * TPAD * width * back.shape[0],
            bytes_accessed=4 << 20,
            transcendentals=0,
        ),
        name="combine",
    )(stream, high, low, back)


def local(
    queries,
    keys,
    values,
    resid,
    w_out,
    w_merge,
    rms_gain,
    w_gate,
    w_up,
    w_down,
    tile_count,
    routes,
    route_weight,
):
    tokens = routes.shape[0]
    position = lax.axis_index("y") * lax.axis_size("x") + lax.axis_index("x")
    page = position // MAXT
    count = lax.dynamic_index_in_dim(tile_count[0], page, keepdims=False)
    live = position % MAXT < count

    half = w_merge.shape[0] // 2
    piece = lax.dynamic_slice_in_dim(w_merge.T, lax.axis_index("core") * half, half, 1)
    piece = lax.all_gather(piece, "x", axis=0, tiled=True)
    merger = lax.all_gather(piece, ("core", "y"), axis=0, tiled=True)
    merger = merger.reshape(2, -1, half)

    table, high, low = slot_tables(routes, route_weight)
    vis = tile_attention(queries, keys, values, resid, w_out)
    merged = jnp.where(live, space_to_depth(vis), jnp.zeros((), jnp.bfloat16))
    merged = jnp.pad(merged, ((0, TPAD - tokens), (0, 0)))

    mine = jnp.concatenate([w_gate[0], w_up[0], w_down[0].T], axis=1)
    mine, merger, merged, table, high, low = lax.optimization_barrier(
        (mine, merger, merged, table, high, low)
    )
    experts = lax.all_gather(mine, ("z", "core"), axis=0, tiled=True)
    stream, send = merge_dispatch(merged, merger, table)
    received = lax.all_to_all(send, ("y", "x"), split_axis=0, concat_axis=0)
    width = stream.shape[1]
    outcome = expert_ffn(received.reshape(-1, width), rms_gain[None, :], experts)
    back = lax.all_to_all(
        outcome.reshape(EXPERTS, SLOT, width), ("y", "x"), split_axis=0, concat_axis=0
    )
    return combine(stream, high, low, back.reshape(-1, width), tokens)


def solution(mesh):
    inner = Mesh(mesh.devices.reshape(8, 2, 8, 4), ("z", "core", "y", "x"))
    pages = ("z", "core")
    expert = ("y", "x")
    rows = P(("z", "core", "y", "x"), None)
    return jax.shard_map(
        local,
        mesh=inner,
        in_specs=(
            rows,
            rows,
            rows,
            rows,
            P(),
            P(None, expert),
            P(),
            P(expert, pages, None),
            P(expert, pages, None),
            P(expert, None, pages),
            P(pages, None),
            rows,
            rows,
        ),
        out_specs=rows,
        check_vma=False,
    )
```

```python
import functools
import jax
import jax.numpy as jnp
from jax import lax
from jax.experimental import pallas as pl
from jax.experimental.pallas import tpu as pltpu
from jax.sharding import Mesh
from jax.sharding import PartitionSpec as P

HEADS = 8
TS = 22
EXPERTS = 32
TOPK = 6
MAXT = 4
SLOT = 32
TPAD = 128


def tile_attention(queries, keys, values, resid, w_out):
    patches = queries.shape[0]
    head_size = queries.shape[1] // HEADS
    q_heads = queries.reshape(patches, HEADS, head_size)
    k_heads = keys.reshape(patches, HEADS, head_size)
    v_heads = values.reshape(patches, HEADS, head_size)
    scores = jnp.einsum(
        "qhd,khd->hqk", q_heads, k_heads, preferred_element_type=jnp.float32
    ) * head_size ** (-0.5)
    top = jnp.max(scores, axis=-1, keepdims=True)
    weights = jnp.exp(scores - top)
    probs = (weights / jnp.sum(weights, axis=-1, keepdims=True)).astype(jnp.bfloat16)
    attended = jnp.einsum(
        "hqk,khd->qhd", probs, v_heads, preferred_element_type=jnp.float32
    ).astype(jnp.bfloat16)
    update = jnp.dot(attended.reshape(patches, -1), w_out, preferred_element_type=jnp.float32)
    return (resid.astype(jnp.float32) + update).astype(jnp.bfloat16)


def space_to_depth(vis):
    half = TS // 2
    width = vis.shape[1]
    grid = vis.reshape(half, 2, half, 2, width).transpose(0, 2, 1, 3, 4)
    return grid.reshape(half * half, 4 * width)


def shift(size, step):
    return [(i, (i + step) % size) for i in range(size)]


def far_shift(size):
    return [(i, (i + (2 if i % 2 == 0 else -2)) % size) for i in range(size)]


def back_again(pairs):
    return [(b, a) for a, b in pairs]


def slot_tables(info, ids):
    tiles = info.shape[0]
    hit = info[:, :TOPK, None, :].astype(jnp.int32) == ids[None, None, :, None]
    member = jnp.any(hit, axis=1)
    weight = jnp.sum(jnp.where(hit, info[:, TOPK : 2 * TOPK, None, :], 0.0), axis=1)
    earlier = jnp.triu(jnp.ones((TPAD, TPAD), jnp.bfloat16), 1)
    before = jnp.dot(
        member.astype(jnp.bfloat16), earlier, preferred_element_type=jnp.float32
    ).astype(jnp.int32)
    place = jnp.where(member, before, -1)
    table = place[:, :, None, :] == jnp.arange(SLOT, dtype=jnp.int32)[None, None, :, None]
    high = weight.astype(jnp.bfloat16)
    low = (weight - high.astype(jnp.float32)).astype(jnp.bfloat16)
    zero = jnp.zeros((), jnp.bfloat16)
    shape = (tiles, ids.shape[0] * SLOT, TPAD)
    parts = [
        jnp.where(table, part[:, :, None, :], zero).reshape(shape).swapaxes(1, 2)
        for part in (high, low)
    ]
    return table.astype(jnp.bfloat16).reshape(shape), jnp.concatenate(parts, axis=1)


def merge_body(merged_ref, weight_ref, stream_ref):
    half = weight_ref.shape[2]
    dims = (((1,), (1,)), ((), ()))
    product = lax.dot_general(
        merged_ref[:, :half], weight_ref[0], dims, preferred_element_type=jnp.float32
    ) + lax.dot_general(
        merged_ref[:, half:], weight_ref[1], dims, preferred_element_type=jnp.float32
    )
    gelu = 0.5 * product * (1.0 + lax.erf(product * (0.5**0.5)))
    stream_ref[...] = gelu.astype(jnp.bfloat16)


def merge(merged, weight):
    width = weight.shape[1]
    block = 256
    return pl.pallas_call(
        merge_body,
        grid=(width // block,),
        in_specs=[
            pl.BlockSpec(merged.shape, lambda i: (0, 0)),
            pl.BlockSpec((2, block, weight.shape[2]), lambda i: (0, i, 0)),
        ],
        out_specs=pl.BlockSpec((TPAD, block), lambda i: (0, i)),
        out_shape=jax.ShapeDtypeStruct((TPAD, width), jnp.bfloat16),
        compiler_params=pltpu.CompilerParams(vmem_limit_bytes=60 << 20),
        cost_estimate=pl.CostEstimate(
            flops=2 * TPAD * width * merged.shape[1],
            bytes_accessed=7 << 20,
            transcendentals=TPAD * width,
        ),
        name="merge",
    )(merged, weight)


def pick_body(table_ref, *refs):
    send_ref = refs[-1]
    cols, hosted, _, slot, width = send_ref.shape
    for i, tile_ref in enumerate(refs[:-1]):
        rows = jnp.dot(table_ref[i], tile_ref[...], preferred_element_type=jnp.float32)
        send_ref[:, :, i] = rows.astype(jnp.bfloat16).reshape(cols, hosted, slot, width)


def pick_rows(table, tiles, cols, hosted):
    width = tiles[0].shape[1]
    block = 256
    count = len(tiles)
    return pl.pallas_call(
        pick_body,
        grid=(width // block,),
        in_specs=[pl.BlockSpec(table.shape, lambda i: (0, 0, 0))]
        + [pl.BlockSpec((TPAD, block), lambda i: (0, i))] * count,
        out_specs=pl.BlockSpec((cols, hosted, count, SLOT, block), lambda i: (0, 0, 0, 0, i)),
        out_shape=jax.ShapeDtypeStruct((cols, hosted, count, SLOT, width), jnp.bfloat16),
        compiler_params=pltpu.CompilerParams(vmem_limit_bytes=60 << 20),
        cost_estimate=pl.CostEstimate(
            flops=2 * TPAD * width * count * table.shape[1],
            bytes_accessed=5 << 20,
            transcendentals=0,
        ),
        name="pick_rows",
    )(table, *tiles)


def expert_body(hidden, main, rows_ref, gain_ref, weight_ref, out_ref):
    width = rows_ref.shape[-1]
    wide = rows_ref[...].reshape(-1, width).astype(jnp.float32)
    scale = lax.rsqrt(jnp.mean(wide * wide, axis=-1, keepdims=True) + 1e-06)
    normed = (wide * scale * gain_ref[...]).astype(jnp.bfloat16)
    both = jnp.dot(normed, weight_ref[:, : 2 * hidden], preferred_element_type=jnp.float32)

    def gated(gate, up):
        return (gate / (1.0 + jnp.exp(-gate)) * up).astype(jnp.bfloat16)

    rest = hidden - main
    act = jnp.concatenate(
        [
            gated(both[:, :main], both[:, main : 2 * main]),
            gated(both[:, 2 * main : 2 * main + rest], both[:, 2 * main + rest :]),
        ],
        axis=1,
    )
    out_ref[...] = (
        lax.dot_general(
            act,
            weight_ref[:, 2 * hidden : 3 * hidden],
            (((1,), (1,)), ((), ())),
            preferred_element_type=jnp.float32,
        )
        .astype(jnp.bfloat16)
        .reshape(out_ref.shape)
    )


def expert_ffn(rows, gain, weight, hidden, main):
    cols, hosted, count, width = rows.shape
    place = lambda j: (0, j, 0, 0)
    return pl.pallas_call(
        functools.partial(expert_body, hidden, main),
        grid=(hosted,),
        in_specs=[
            pl.BlockSpec((cols, 1, count, width), place),
            pl.BlockSpec((1, width), lambda j: (0, 0)),
            pl.BlockSpec((width, weight.shape[1] // hosted), lambda j: (0, j)),
        ],
        out_specs=pl.BlockSpec((cols, 1, count, width), place),
        out_shape=jax.ShapeDtypeStruct(rows.shape, jnp.bfloat16),
        compiler_params=pltpu.CompilerParams(vmem_limit_bytes=60 << 20),
        cost_estimate=pl.CostEstimate(
            flops=6 * cols * hosted * count * width * hidden,
            bytes_accessed=16 << 20,
            transcendentals=cols * hosted * count * hidden,
        ),
        name="expert_ffn",
    )(rows, gain, weight)


def combine_body(base, mix_ref, back_ref, *refs):
    for i, out_ref in enumerate(refs):
        back = back_ref[:, :, base + i].reshape(mix_ref.shape[2], out_ref.shape[1])
        both = jnp.dot(mix_ref[base + i], back, preferred_element_type=jnp.float32)
        out_ref[...] = (both[:TPAD] + both[TPAD:]).astype(out_ref.dtype)


def combine(mix, back, base, count, dtype):
    cols, hosted, tiles, slot, width = back.shape
    block = 256
    return pl.pallas_call(
        functools.partial(combine_body, base),
        grid=(width // block,),
        in_specs=[
            pl.BlockSpec(mix.shape, lambda i: (0, 0, 0)),
            pl.BlockSpec((cols, hosted, tiles, slot, block), lambda i: (0, 0, 0, 0, i)),
        ],
        out_specs=[pl.BlockSpec((TPAD, block), lambda i: (0, i))] * count,
        out_shape=[jax.ShapeDtypeStruct((TPAD, width), dtype)] * count,
        compiler_params=pltpu.CompilerParams(vmem_limit_bytes=60 << 20),
        cost_estimate=pl.CostEstimate(
            flops=4 * TPAD * width * count * mix.shape[2],
            bytes_accessed=4 << 20,
            transcendentals=0,
        ),
        name="combine",
    )(mix, back)


def local(
    queries,
    keys,
    values,
    resid,
    w_out,
    w_merge,
    rms_gain,
    w_gate,
    w_up,
    w_down,
    tile_count,
    routes,
    route_weight,
):
    tokens = routes.shape[0]
    hidden = w_gate.shape[2]
    rows = lax.axis_size("y")
    cols = lax.axis_size("x")
    row = lax.axis_index("y")
    position = row * cols + lax.axis_index("x")
    page = position // MAXT
    count = lax.dynamic_index_in_dim(tile_count[0], page, keepdims=False)
    live = position % MAXT < count

    half = w_merge.shape[0] // 2
    piece = lax.dynamic_slice_in_dim(w_merge.T, lax.axis_index("core") * half, half, 1)
    piece = lax.all_gather(piece, "x", axis=0, tiled=True)

    edge = -(-3 * hidden // 128) * 128 - 3 * hidden
    main = hidden // 128 * 128
    gate, up, down = w_gate[0], w_up[0], w_down[0].T
    blank = jnp.zeros((down.shape[0], edge), down.dtype)
    own = jnp.concatenate(
        [gate[:, :main], up[:, :main], gate[:, main:], up[:, main:], down, blank], axis=1
    )
    routing = jnp.concatenate(
        [
            jnp.pad(routes, ((0, TPAD - tokens), (0, 0)), constant_values=-1).astype(jnp.float32),
            jnp.pad(route_weight, ((0, TPAD - tokens), (0, 0))),
        ],
        axis=1,
    ).T
    piece, own, routing = lax.optimization_barrier((piece, own, routing))
    merger = lax.all_gather(piece, ("core", "y"), axis=0, tiled=True)
    merger = merger.reshape(2, -1, half)
    other = lax.ppermute(own, "y", shift(rows, rows // 2))
    steps = (shift(rows, 1), shift(rows, -1), far_shift(rows))
    info = jnp.stack([routing] + [lax.ppermute(routing, "y", step) for step in steps])
    hosted = jnp.stack([row, (row + rows // 2) % rows])
    ids = (hosted[None, :] * cols + jnp.arange(cols, dtype=jnp.int32)[:, None]).reshape(-1)
    table, mix = slot_tables(info, ids)

    vis = tile_attention(queries, keys, values, resid, w_out)
    merged = jnp.where(live, space_to_depth(vis), jnp.zeros((), jnp.bfloat16))
    merged = jnp.pad(merged, ((0, TPAD - tokens), (0, 0)))

    mine = jnp.concatenate([own, other], axis=1)
    mine, merger, merged, table, mix = lax.optimization_barrier(
        (mine, merger, merged, table, mix)
    )
    experts = lax.all_gather(mine, ("z", "core"), axis=0, tiled=True)

    stream = merge(merged, merger)
    width = stream.shape[1]
    tiles = [stream] + [lax.ppermute(stream, "y", step) for step in steps]
    send = pick_rows(table, tiles, cols, 2)
    flat = (cols, send.size // cols // width, width)
    received = lax.all_to_all(send.reshape(flat), "x", split_axis=0, concat_axis=0)
    outcome = expert_ffn(
        received.reshape(cols, 2, -1, width), rms_gain[None, :], experts, hidden, main
    )
    back = lax.all_to_all(outcome.reshape(flat), "x", split_axis=0, concat_axis=0)
    back = back.reshape(send.shape)
    parts = combine(mix, back, 1, len(steps), jnp.bfloat16)
    total = combine(mix, back, 0, 1, jnp.float32)[0] + stream.astype(jnp.float32)
    for part, step in zip(parts, steps):
        total = total + lax.ppermute(part, "y", back_again(step)).astype(jnp.float32)
    return total[:tokens].astype(jnp.bfloat16)


def solution(mesh):
    inner = Mesh(mesh.devices.reshape(8, 2, 8, 4), ("z", "core", "y", "x"))
    pages = ("z", "core")
    expert = ("y", "x")
    rows = P(("z", "core", "y", "x"), None)
    return jax.shard_map(
        local,
        mesh=inner,
        in_specs=(
            rows,
            rows,
            rows,
            rows,
            P(),
            P(None, expert),
            P(),
            P(expert, pages, None),
            P(expert, pages, None),
            P(expert, None, pages),
            P(pages, None),
            rows,
            rows,
        ),
        out_specs=rows,
        check_vma=False,
    )
```

```python
import functools
import jax
import jax.numpy as jnp
from jax import lax
from jax.experimental import pallas as pl
from jax.experimental.pallas import tpu as pltpu
from jax.sharding import Mesh
from jax.sharding import PartitionSpec as P

HEADS = 8
TS = 22
EXPERTS = 32
TOPK = 6
MAXT = 4
SLOT = 32
TPAD = 128


def tile_attention(queries, keys, values, resid, w_out):
    patches = queries.shape[0]
    head_size = queries.shape[1] // HEADS
    q_heads = queries.reshape(patches, HEADS, head_size)
    k_heads = keys.reshape(patches, HEADS, head_size)
    v_heads = values.reshape(patches, HEADS, head_size)
    scores = jnp.einsum(
        "qhd,khd->hqk", q_heads, k_heads, preferred_element_type=jnp.float32
    ) * head_size ** (-0.5)
    top = jnp.max(scores, axis=-1, keepdims=True)
    weights = jnp.exp(scores - top)
    probs = (weights / jnp.sum(weights, axis=-1, keepdims=True)).astype(jnp.bfloat16)
    attended = jnp.einsum(
        "hqk,khd->qhd", probs, v_heads, preferred_element_type=jnp.float32
    ).astype(jnp.bfloat16)
    update = jnp.dot(attended.reshape(patches, -1), w_out, preferred_element_type=jnp.float32)
    return (resid.astype(jnp.float32) + update).astype(jnp.bfloat16)


def space_to_depth(vis):
    half = TS // 2
    width = vis.shape[1]
    grid = vis.reshape(half, 2, half, 2, width).transpose(0, 2, 1, 3, 4)
    return grid.reshape(half * half, 4 * width)


def shift(size, step):
    return [(i, (i + step) % size) for i in range(size)]


def far_shift(size):
    return [(i, (i + (2 if i % 2 == 0 else -2)) % size) for i in range(size)]


def back_again(pairs):
    return [(b, a) for a, b in pairs]


def slot_tables(info, ids):
    tiles = info.shape[0]
    hit = info[:, :TOPK, None, :].astype(jnp.int32) == ids[None, None, :, None]
    member = jnp.any(hit, axis=1)
    weight = jnp.sum(jnp.where(hit, info[:, TOPK : 2 * TOPK, None, :], 0.0), axis=1)
    earlier = jnp.triu(jnp.ones((TPAD, TPAD), jnp.bfloat16), 1)
    before = jnp.dot(
        member.astype(jnp.bfloat16), earlier, preferred_element_type=jnp.float32
    ).astype(jnp.int32)
    place = jnp.where(member, before, -1)
    table = place[:, :, None, :] == jnp.arange(SLOT, dtype=jnp.int32)[None, None, :, None]
    high = weight.astype(jnp.bfloat16)
    low = (weight - high.astype(jnp.float32)).astype(jnp.bfloat16)
    zero = jnp.zeros((), jnp.bfloat16)
    shape = (tiles, ids.shape[0] * SLOT, TPAD)
    parts = [
        jnp.where(table, part[:, :, None, :], zero).reshape(shape).swapaxes(1, 2)
        for part in (high, low)
    ]
    return table.astype(jnp.bfloat16).reshape(shape), jnp.concatenate(parts, axis=1)


def merge_body(merged_ref, weight_ref, stream_ref):
    half = weight_ref.shape[2]
    dims = (((1,), (1,)), ((), ()))
    product = lax.dot_general(
        merged_ref[:, :half], weight_ref[0], dims, preferred_element_type=jnp.float32
    ) + lax.dot_general(
        merged_ref[:, half:], weight_ref[1], dims, preferred_element_type=jnp.float32
    )
    gelu = 0.5 * product * (1.0 + lax.erf(product * (0.5**0.5)))
    stream_ref[...] = gelu.astype(jnp.bfloat16)


def merge(merged, weight):
    width = weight.shape[1]
    block = 256
    return pl.pallas_call(
        merge_body,
        grid=(width // block,),
        in_specs=[
            pl.BlockSpec(merged.shape, lambda i: (0, 0)),
            pl.BlockSpec((2, block, weight.shape[2]), lambda i: (0, i, 0)),
        ],
        out_specs=pl.BlockSpec((TPAD, block), lambda i: (0, i)),
        out_shape=jax.ShapeDtypeStruct((TPAD, width), jnp.bfloat16),
        compiler_params=pltpu.CompilerParams(vmem_limit_bytes=60 << 20),
        cost_estimate=pl.CostEstimate(
            flops=2 * TPAD * width * merged.shape[1],
            bytes_accessed=7 << 20,
            transcendentals=TPAD * width,
        ),
        name="merge",
    )(merged, weight)


def pick_body(table_ref, tile_ref, *refs):
    send_ref = refs[-1]
    rows = jnp.dot(table_ref[0], tile_ref[...], preferred_element_type=jnp.float32)
    send_ref[...] = rows.astype(jnp.bfloat16).reshape(send_ref.shape)


def pick_rows(table, index, tile, shape, send=None):
    cols, hosted, _, slot, width = shape
    given = [] if send is None else [send]
    return pl.pallas_call(
        pick_body,
        grid=(1,),
        in_specs=[
            pl.BlockSpec((1,) + table.shape[1:], lambda i: (index, 0, 0)),
            pl.BlockSpec(tile.shape, lambda i: (0, 0)),
        ]
        + [pl.BlockSpec(memory_space=pl.ANY)] * len(given),
        out_specs=pl.BlockSpec((cols, hosted, 1, slot, width), lambda i: (0, 0, index, 0, 0)),
        out_shape=jax.ShapeDtypeStruct(shape, jnp.bfloat16),
        input_output_aliases={2: 0} if given else {},
        compiler_params=pltpu.CompilerParams(vmem_limit_bytes=60 << 20),
        cost_estimate=pl.CostEstimate(
            flops=2 * TPAD * width * table.shape[1],
            bytes_accessed=1 << 20,
            transcendentals=0,
        ),
        name="pick_rows",
    )(table, tile, *given)


def expert_body(hidden, main, rows_any, gain_ref, weight_any, out_any, rows, weight, out, sems):
    cols, hosted, count, width = rows_any.shape
    span = weight_any.shape[1] // hosted
    first = 2 * hidden
    copies = []
    for j in range(hosted):
        copies.append(
            [
                pltpu.make_async_copy(rows_any.at[:, j], rows.at[j], sems.at[j, 0]),
                pltpu.make_async_copy(
                    weight_any.at[:, pl.ds(j * span, first)],
                    weight.at[j, :, pl.ds(0, first)],
                    sems.at[j, 1],
                ),
                pltpu.make_async_copy(
                    weight_any.at[:, pl.ds(j * span + first, span - first)],
                    weight.at[j, :, pl.ds(first, span - first)],
                    sems.at[j, 2],
                ),
            ]
        )
    for group in copies:
        for copy in group:
            copy.start()

    def gated(gate, up):
        return (gate / (1.0 + jnp.exp(-gate)) * up).astype(jnp.bfloat16)

    rest = hidden - main
    results = []
    for j in range(hosted):
        copies[j][0].wait()
        wide = rows[j].reshape(-1, width).astype(jnp.float32)
        scale = lax.rsqrt(jnp.mean(wide * wide, axis=-1, keepdims=True) + 1e-06)
        normed = (wide * scale * gain_ref[...]).astype(jnp.bfloat16)
        copies[j][1].wait()
        both = jnp.dot(normed, weight[j, :, :first], preferred_element_type=jnp.float32)
        act = jnp.concatenate(
            [
                gated(both[:, :main], both[:, main : 2 * main]),
                gated(both[:, 2 * main : 2 * main + rest], both[:, 2 * main + rest :]),
            ],
            axis=1,
        )
        copies[j][2].wait()
        out[j] = (
            lax.dot_general(
                act,
                weight[j, :, first : first + hidden],
                (((1,), (1,)), ((), ())),
                preferred_element_type=jnp.float32,
            )
            .astype(jnp.bfloat16)
            .reshape(cols, count, width)
        )
        result = pltpu.make_async_copy(out.at[j], out_any.at[:, j], sems.at[j, 3])
        result.start()
        results.append(result)
    for result in results:
        result.wait()


def expert_ffn(rows, gain, weight, hidden, main):
    cols, hosted, count, width = rows.shape
    held = (hosted, cols, count, width)
    anywhere = pl.BlockSpec(memory_space=pl.ANY)
    return pl.pallas_call(
        functools.partial(expert_body, hidden, main),
        in_specs=[anywhere, pl.BlockSpec(memory_space=pltpu.VMEM), anywhere],
        out_specs=anywhere,
        out_shape=jax.ShapeDtypeStruct(rows.shape, jnp.bfloat16),
        scratch_shapes=[
            pltpu.VMEM(held, jnp.bfloat16),
            pltpu.VMEM((hosted, width, weight.shape[1] // hosted), jnp.bfloat16),
            pltpu.VMEM(held, jnp.bfloat16),
            pltpu.SemaphoreType.DMA((hosted, 4)),
        ],
        compiler_params=pltpu.CompilerParams(vmem_limit_bytes=60 << 20),
        cost_estimate=pl.CostEstimate(
            flops=6 * cols * hosted * count * width * hidden,
            bytes_accessed=16 << 20,
            transcendentals=cols * hosted * count * hidden,
        ),
        name="expert_ffn",
    )(rows, gain, weight)


def combine_body(mix_ref, back_ref, out_ref):
    back = back_ref[...].reshape(mix_ref.shape[2], out_ref.shape[1])
    both = jnp.dot(mix_ref[0], back, preferred_element_type=jnp.float32)
    out_ref[...] = (both[:TPAD] + both[TPAD:]).astype(out_ref.dtype)


def combine(mix, back, index, dtype):
    cols, hosted, _, slot, width = back.shape
    return pl.pallas_call(
        combine_body,
        grid=(1,),
        in_specs=[
            pl.BlockSpec((1,) + mix.shape[1:], lambda i: (index, 0, 0)),
            pl.BlockSpec((cols, hosted, 1, slot, width), lambda i: (0, 0, index, 0, 0)),
        ],
        out_specs=pl.BlockSpec((TPAD, width), lambda i: (0, 0)),
        out_shape=jax.ShapeDtypeStruct((TPAD, width), dtype),
        compiler_params=pltpu.CompilerParams(vmem_limit_bytes=24 << 20),
        cost_estimate=pl.CostEstimate(
            flops=4 * TPAD * width * mix.shape[2],
            bytes_accessed=1 << 20,
            transcendentals=0,
        ),
        name="combine",
    )(mix, back)


def local(
    queries,
    keys,
    values,
    resid,
    w_out,
    w_merge,
    rms_gain,
    w_gate,
    w_up,
    w_down,
    tile_count,
    routes,
    route_weight,
):
    tokens = routes.shape[0]
    hidden = w_gate.shape[2]
    rows = lax.axis_size("y")
    cols = lax.axis_size("x")
    row = lax.axis_index("y")
    position = row * cols + lax.axis_index("x")
    page = position // MAXT
    count = lax.dynamic_index_in_dim(tile_count[0], page, keepdims=False)
    live = position % MAXT < count

    half = w_merge.shape[0] // 2
    piece = lax.dynamic_slice_in_dim(w_merge.T, lax.axis_index("core") * half, half, 1)
    piece = lax.all_to_all(
        jnp.broadcast_to(piece[None], (cols,) + piece.shape), "x", split_axis=0, concat_axis=0
    )
    piece = piece.reshape(-1, half)
    queries, w_gate, w_up, w_down, routes, route_weight, piece = lax.optimization_barrier(
        (queries, w_gate, w_up, w_down, routes, route_weight, piece)
    )
    merger = lax.all_gather(piece, ("core", "y"), axis=0, tiled=True)
    merger = merger.reshape(2, -1, half)

    edge = -(-3 * hidden // 128) * 128 - 3 * hidden
    main = hidden // 128 * 128
    gate, up, down = w_gate[0], w_up[0], w_down[0].T
    blank = jnp.zeros((down.shape[0], edge), down.dtype)
    own = jnp.concatenate(
        [gate[:, :main], up[:, :main], gate[:, main:], up[:, main:], down, blank], axis=1
    )
    routing = jnp.concatenate(
        [
            jnp.pad(routes, ((0, TPAD - tokens), (0, 0)), constant_values=-1).astype(jnp.float32),
            jnp.pad(route_weight, ((0, TPAD - tokens), (0, 0))),
        ],
        axis=1,
    ).T
    middle = own.shape[0] // 2
    ways = []
    for part, step in ((own[:middle], rows // 4), (own[middle:], -(rows // 4))):
        for _ in range(2):
            part = lax.ppermute(part, "y", shift(rows, step))
        ways.append(part)
    other = jnp.concatenate(ways, axis=0)
    steps = (shift(rows, 1), shift(rows, -1), far_shift(rows))
    info = jnp.stack([routing] + [lax.ppermute(routing, "y", step) for step in steps])
    hosted = jnp.stack([row, (row + rows // 2) % rows])
    ids = (hosted[None, :] * cols + jnp.arange(cols, dtype=jnp.int32)[:, None]).reshape(-1)
    table, mix = slot_tables(info, ids)

    vis = tile_attention(queries, keys, values, resid, w_out)
    merged = jnp.where(live, space_to_depth(vis), jnp.zeros((), jnp.bfloat16))
    merged = jnp.pad(merged, ((0, TPAD - tokens), (0, 0)))

    mine = jnp.concatenate([own, other], axis=1)
    mine, merger, merged, table, mix = lax.optimization_barrier(
        (mine, merger, merged, table, mix)
    )
    experts = lax.all_gather(mine, ("z", "core"), axis=0, tiled=True)

    stream = merge(merged, merger)
    width = stream.shape[1]
    shape = (cols, 2, 1 + len(steps), SLOT, width)
    arrived = [lax.ppermute(stream, "y", step) for step in steps]
    send = pick_rows(table, 0, stream, shape)
    for i, tile in enumerate(arrived):
        send = pick_rows(table, i + 1, tile, shape, send)
    flat = (cols, send.size // cols // width, width)
    received = lax.all_to_all(send.reshape(flat), "x", split_axis=0, concat_axis=0)
    outcome = expert_ffn(
        received.reshape(cols, 2, -1, width), rms_gain[None, :], experts, hidden, main
    )
    back = lax.all_to_all(outcome.reshape(flat), "x", split_axis=0, concat_axis=0)
    back = back.reshape(shape)
    parts = [
        lax.ppermute(combine(mix, back, i + 1, jnp.bfloat16), "y", back_again(step))
        for i, step in enumerate(steps)
    ]
    total = combine(mix, back, 0, jnp.float32) + stream.astype(jnp.float32)
    for part in parts:
        total = total + part.astype(jnp.float32)
    return total[:tokens].astype(jnp.bfloat16)


def solution(mesh):
    inner = Mesh(mesh.devices.reshape(8, 2, 8, 4), ("z", "core", "y", "x"))
    pages = ("z", "core")
    expert = ("y", "x")
    rows = P(("z", "core", "y", "x"), None)
    return jax.shard_map(
        local,
        mesh=inner,
        in_specs=(
            rows,
            rows,
            rows,
            rows,
            P(),
            P(None, expert),
            P(),
            P(expert, pages, None),
            P(expert, pages, None),
            P(expert, None, pages),
            P(pages, None),
            rows,
            rows,
        ),
        out_specs=rows,
        check_vma=False,
    )
```

```python
import functools
import jax
import jax.numpy as jnp
from jax import lax
from jax.experimental import pallas as pl
from jax.experimental.pallas import tpu as pltpu
from jax.sharding import Mesh
from jax.sharding import PartitionSpec as P

HEADS = 8
TS = 22
EXPERTS = 32
TOPK = 6
MAXT = 4
SLOT = 32
TPAD = 128


def tile_attention(queries, keys, values, resid, w_out):
    patches = queries.shape[0]
    head_size = queries.shape[1] // HEADS
    q_heads = queries.reshape(patches, HEADS, head_size)
    k_heads = keys.reshape(patches, HEADS, head_size)
    v_heads = values.reshape(patches, HEADS, head_size)
    scores = jnp.einsum(
        "qhd,khd->hqk", q_heads, k_heads, preferred_element_type=jnp.float32
    ) * head_size ** (-0.5)
    top = jnp.max(scores, axis=-1, keepdims=True)
    weights = jnp.exp(scores - top)
    probs = (weights / jnp.sum(weights, axis=-1, keepdims=True)).astype(jnp.bfloat16)
    attended = jnp.einsum(
        "hqk,khd->qhd", probs, v_heads, preferred_element_type=jnp.float32
    ).astype(jnp.bfloat16)
    update = jnp.dot(attended.reshape(patches, -1), w_out, preferred_element_type=jnp.float32)
    return (resid.astype(jnp.float32) + update).astype(jnp.bfloat16)


def space_to_depth(vis):
    half = TS // 2
    width = vis.shape[1]
    grid = vis.reshape(half, 2, half, 2, width).transpose(0, 2, 1, 3, 4)
    return grid.reshape(half * half, 4 * width)


def shift(size, step):
    return [(i, (i + step) % size) for i in range(size)]


def far_shift(size):
    return [(i, (i + (2 if i % 2 == 0 else -2)) % size) for i in range(size)]


def back_again(pairs):
    return [(b, a) for a, b in pairs]


def slot_tables(info, ids):
    tiles = info.shape[0]
    hit = info[:, :TOPK, None, :].astype(jnp.int32) == ids[None, None, :, None]
    member = jnp.any(hit, axis=1)
    weight = jnp.sum(jnp.where(hit, info[:, TOPK : 2 * TOPK, None, :], 0.0), axis=1)
    earlier = jnp.triu(jnp.ones((TPAD, TPAD), jnp.bfloat16), 1)
    before = jnp.dot(
        member.astype(jnp.bfloat16), earlier, preferred_element_type=jnp.float32
    ).astype(jnp.int32)
    place = jnp.where(member, before, -1)
    table = place[:, :, None, :] == jnp.arange(SLOT, dtype=jnp.int32)[None, None, :, None]
    high = weight.astype(jnp.bfloat16)
    low = (weight - high.astype(jnp.float32)).astype(jnp.bfloat16)
    zero = jnp.zeros((), jnp.bfloat16)
    shape = (tiles, ids.shape[0] * SLOT, TPAD)
    parts = [
        jnp.where(table, part[:, :, None, :], zero).reshape(shape).swapaxes(1, 2)
        for part in (high, low)
    ]
    return table.astype(jnp.bfloat16).reshape(shape), jnp.concatenate(parts, axis=1)


def merge_body(merged_ref, weight_ref, stream_ref):
    half = weight_ref.shape[2]
    dims = (((1,), (1,)), ((), ()))
    product = lax.dot_general(
        merged_ref[:, :half], weight_ref[0], dims, preferred_element_type=jnp.float32
    ) + lax.dot_general(
        merged_ref[:, half:], weight_ref[1], dims, preferred_element_type=jnp.float32
    )
    gelu = 0.5 * product * (1.0 + lax.erf(product * (0.5**0.5)))
    stream_ref[...] = gelu.astype(jnp.bfloat16)


def merge(merged, weight):
    width = weight.shape[1]
    block = 256
    return pl.pallas_call(
        merge_body,
        grid=(width // block,),
        in_specs=[
            pl.BlockSpec(merged.shape, lambda i: (0, 0)),
            pl.BlockSpec((2, block, weight.shape[2]), lambda i: (0, i, 0)),
        ],
        out_specs=pl.BlockSpec((TPAD, block), lambda i: (0, i)),
        out_shape=jax.ShapeDtypeStruct((TPAD, width), jnp.bfloat16),
        compiler_params=pltpu.CompilerParams(vmem_limit_bytes=60 << 20),
        cost_estimate=pl.CostEstimate(
            flops=2 * TPAD * width * merged.shape[1],
            bytes_accessed=7 << 20,
            transcendentals=TPAD * width,
        ),
        name="merge",
    )(merged, weight)


def pick_body(index, table_ref, tile_ref, *refs):
    send, rows, sem = refs[-3:]
    picked = jnp.dot(table_ref[0], tile_ref[...], preferred_element_type=jnp.float32)
    rows[...] = picked.astype(jnp.bfloat16).reshape(rows.shape)
    copy = pltpu.make_async_copy(rows, send.at[:, :, index], sem)
    copy.start()
    copy.wait()


def pick_rows(table, index, tile, shape, send=None):
    cols, hosted, _, slot, width = shape
    given = [] if send is None else [send]
    return pl.pallas_call(
        functools.partial(pick_body, index),
        grid=(1,),
        in_specs=[
            pl.BlockSpec((1,) + table.shape[1:], lambda i: (index, 0, 0)),
            pl.BlockSpec(tile.shape, lambda i: (0, 0)),
        ]
        + [pl.BlockSpec(memory_space=pltpu.HBM)] * len(given),
        out_specs=pl.BlockSpec(memory_space=pltpu.HBM),
        out_shape=jax.ShapeDtypeStruct(shape, jnp.bfloat16),
        scratch_shapes=[
            pltpu.VMEM((cols, hosted, slot, width), jnp.bfloat16),
            pltpu.SemaphoreType.DMA,
        ],
        input_output_aliases={2: 0} if given else {},
        compiler_params=pltpu.CompilerParams(vmem_limit_bytes=24 << 20),
        cost_estimate=pl.CostEstimate(
            flops=2 * TPAD * width * table.shape[1],
            bytes_accessed=1 << 20,
            transcendentals=0,
        ),
        name="pick_rows",
    )(table, tile, *given)


def expert_body(hidden, rows_hbm, gain_ref, weight_hbm, out_hbm, rows, weight, out, sems):
    cols, hosted, count, width = rows_hbm.shape
    span = weight_hbm.shape[1] // hosted
    first = 2 * hidden

    def load(j):
        copies = [
            pltpu.make_async_copy(rows_hbm.at[:, j], rows.at[j], sems.at[j, 0]),
            pltpu.make_async_copy(
                weight_hbm.at[:, pl.ds(j * span, first)],
                weight.at[j, :, pl.ds(0, first)],
                sems.at[j, 1],
            ),
            pltpu.make_async_copy(
                weight_hbm.at[:, pl.ds(j * span + first, span - first)],
                weight.at[j, :, pl.ds(first, span - first)],
                sems.at[j, 2],
            ),
        ]
        for copy in copies:
            copy.start()
        return copies

    pending = load(0)
    results = []
    for j in range(hosted):
        current = pending
        current[0].wait()
        wide = rows[j].reshape(-1, width).astype(jnp.float32)
        scale = lax.rsqrt(jnp.mean(wide * wide, axis=-1, keepdims=True) + 1e-06)
        normed = (wide * scale * gain_ref[...]).astype(jnp.bfloat16)
        current[1].wait()
        if j + 1 < hosted:
            pending = load(j + 1)
        both = jnp.dot(normed, weight[j, :, :first], preferred_element_type=jnp.float32)
        gate = both[:, :hidden]
        up = both[:, hidden:]
        act = (gate / (1.0 + jnp.exp(-gate)) * up).astype(jnp.bfloat16)
        current[2].wait()
        out[j] = (
            lax.dot_general(
                act,
                weight[j, :, first : first + hidden],
                (((1,), (1,)), ((), ())),
                preferred_element_type=jnp.float32,
            )
            .astype(jnp.bfloat16)
            .reshape(cols, count, width)
        )
        result = pltpu.make_async_copy(out.at[j], out_hbm.at[:, j], sems.at[j, 3])
        result.start()
        results.append(result)
    for result in results:
        result.wait()


def expert_ffn(rows, gain, weight, hidden):
    cols, hosted, count, width = rows.shape
    held = (hosted, cols, count, width)
    hbm = pl.BlockSpec(memory_space=pltpu.HBM)
    return pl.pallas_call(
        functools.partial(expert_body, hidden),
        in_specs=[hbm, pl.BlockSpec(memory_space=pltpu.VMEM), hbm],
        out_specs=hbm,
        out_shape=jax.ShapeDtypeStruct(rows.shape, jnp.bfloat16),
        scratch_shapes=[
            pltpu.VMEM(held, jnp.bfloat16),
            pltpu.VMEM((hosted, width, weight.shape[1] // hosted), jnp.bfloat16),
            pltpu.VMEM(held, jnp.bfloat16),
            pltpu.SemaphoreType.DMA((hosted, 4)),
        ],
        compiler_params=pltpu.CompilerParams(vmem_limit_bytes=60 << 20),
        cost_estimate=pl.CostEstimate(
            flops=6 * cols * hosted * count * width * hidden,
            bytes_accessed=16 << 20,
            transcendentals=cols * hosted * count * hidden,
        ),
        name="expert_ffn",
    )(rows, gain, weight)


def combine_body(mix_ref, back_ref, out_ref):
    back = back_ref[...].reshape(mix_ref.shape[2], out_ref.shape[1])
    both = jnp.dot(mix_ref[0], back, preferred_element_type=jnp.float32)
    out_ref[...] = (both[:TPAD] + both[TPAD:]).astype(out_ref.dtype)


def combine(mix, back, index, dtype):
    cols, hosted, _, slot, width = back.shape
    return pl.pallas_call(
        combine_body,
        grid=(1,),
        in_specs=[
            pl.BlockSpec((1,) + mix.shape[1:], lambda i: (index, 0, 0)),
            pl.BlockSpec((cols, hosted, 1, slot, width), lambda i: (0, 0, index, 0, 0)),
        ],
        out_specs=pl.BlockSpec((TPAD, width), lambda i: (0, 0)),
        out_shape=jax.ShapeDtypeStruct((TPAD, width), dtype),
        compiler_params=pltpu.CompilerParams(vmem_limit_bytes=24 << 20),
        cost_estimate=pl.CostEstimate(
            flops=4 * TPAD * width * mix.shape[2],
            bytes_accessed=1 << 20,
            transcendentals=0,
        ),
        name="combine",
    )(mix, back)


def local(
    queries,
    keys,
    values,
    resid,
    w_out,
    w_merge,
    rms_gain,
    w_gate,
    w_up,
    w_down,
    tile_count,
    routes,
    route_weight,
):
    tokens = routes.shape[0]
    hidden = w_gate.shape[2]
    rows = lax.axis_size("y")
    cols = lax.axis_size("x")
    row = lax.axis_index("y")
    position = row * cols + lax.axis_index("x")
    page = position // MAXT
    count = lax.dynamic_index_in_dim(tile_count[0], page, keepdims=False)
    live = position % MAXT < count

    half = w_merge.shape[0] // 2
    piece = lax.dynamic_slice_in_dim(w_merge.T, lax.axis_index("core") * half, half, 1)
    down = w_down[0].T
    blank = jnp.zeros((down.shape[0], -(-3 * hidden // 128) * 128 - 3 * hidden), down.dtype)
    own = jnp.concatenate([w_gate[0], w_up[0], down, blank], axis=1)
    own, piece = lax.optimization_barrier((own, piece))
    other = lax.ppermute(own, "y", shift(rows, rows // 2))
    piece = lax.all_to_all(
        jnp.broadcast_to(piece[None], (cols,) + piece.shape), "x", split_axis=0, concat_axis=0
    )
    piece = piece.reshape(-1, half)
    queries, routes, route_weight, piece, own, other = lax.optimization_barrier(
        (queries, routes, route_weight, piece, own, other)
    )
    merger = lax.all_gather(piece, ("core", "y"), axis=0, tiled=True)
    merger = merger.reshape(2, -1, half)

    routing = jnp.concatenate(
        [
            jnp.pad(routes, ((0, TPAD - tokens), (0, 0)), constant_values=-1).astype(jnp.float32),
            jnp.pad(route_weight, ((0, TPAD - tokens), (0, 0))),
        ],
        axis=1,
    ).T
    steps = (shift(rows, 1), shift(rows, -1), far_shift(rows))
    info = jnp.stack([routing] + [lax.ppermute(routing, "y", step) for step in steps])
    hosted = jnp.stack([row, (row + rows // 2) % rows])
    ids = (hosted[None, :] * cols + jnp.arange(cols, dtype=jnp.int32)[:, None]).reshape(-1)
    table, mix = slot_tables(info, ids)

    vis = tile_attention(queries, keys, values, resid, w_out)
    merged = jnp.where(live, space_to_depth(vis), jnp.zeros((), jnp.bfloat16))
    merged = jnp.pad(merged, ((0, TPAD - tokens), (0, 0)))

    mine = jnp.concatenate([own, other], axis=1)
    mine, merger, merged, table, mix = lax.optimization_barrier(
        (mine, merger, merged, table, mix)
    )
    experts = lax.all_gather(mine, ("z", "core"), axis=0, tiled=True)

    stream = merge(merged, merger)
    width = stream.shape[1]
    shape = (cols, 2, 1 + len(steps), SLOT, width)
    arrived = [lax.ppermute(stream, "y", step) for step in steps]
    send = pick_rows(table, 0, stream, shape)
    for i, tile in enumerate(arrived):
        send = pick_rows(table, i + 1, tile, shape, send)
    flat = (cols, send.size // cols // width, width)
    received = lax.all_to_all(send.reshape(flat), "x", split_axis=0, concat_axis=0)
    outcome = expert_ffn(
        received.reshape(cols, 2, -1, width),
        rms_gain[None, :],
        experts,
        hidden,
    )
    back = lax.all_to_all(outcome.reshape(flat), "x", split_axis=0, concat_axis=0)
    back = back.reshape(shape)
    parts = [
        lax.ppermute(combine(mix, back, i + 1, jnp.bfloat16), "y", back_again(step))
        for i, step in enumerate(steps)
    ]
    total = combine(mix, back, 0, jnp.float32) + stream.astype(jnp.float32)
    for part in parts:
        total = total + part.astype(jnp.float32)
    return total[:tokens].astype(jnp.bfloat16)


def solution(mesh):
    inner = Mesh(mesh.devices.reshape(8, 2, 8, 4), ("z", "core", "y", "x"))
    pages = ("z", "core")
    expert = ("y", "x")
    rows = P(("z", "core", "y", "x"), None)
    return jax.shard_map(
        local,
        mesh=inner,
        in_specs=(
            rows,
            rows,
            rows,
            rows,
            P(),
            P(None, expert),
            P(),
            P(expert, pages, None),
            P(expert, pages, None),
            P(expert, None, pages),
            P(pages, None),
            rows,
            rows,
        ),
        out_specs=rows,
        check_vma=False,
    )
```

```python
import functools
import jax
import jax.numpy as jnp
from jax import lax
from jax.experimental import pallas as pl
from jax.experimental.pallas import tpu as pltpu
from jax.sharding import Mesh
from jax.sharding import PartitionSpec as P

HEADS = 8
TS = 22
EXPERTS = 32
TOPK = 6
MAXT = 4
SLOT = 32
TPAD = 128


def tile_attention(queries, keys, values, resid, w_out):
    patches = queries.shape[0]
    head_size = queries.shape[1] // HEADS
    q_heads = queries.reshape(patches, HEADS, head_size)
    k_heads = keys.reshape(patches, HEADS, head_size)
    v_heads = values.reshape(patches, HEADS, head_size)
    scores = jnp.einsum(
        "qhd,khd->hqk", q_heads, k_heads, preferred_element_type=jnp.float32
    ) * head_size ** (-0.5)
    top = jnp.max(scores, axis=-1, keepdims=True)
    weights = jnp.exp(scores - top)
    probs = (weights / jnp.sum(weights, axis=-1, keepdims=True)).astype(jnp.bfloat16)
    attended = jnp.einsum(
        "hqk,khd->qhd", probs, v_heads, preferred_element_type=jnp.float32
    ).astype(jnp.bfloat16)
    update = jnp.dot(attended.reshape(patches, -1), w_out, preferred_element_type=jnp.float32)
    return (resid.astype(jnp.float32) + update).astype(jnp.bfloat16)


def space_to_depth(vis):
    half = TS // 2
    width = vis.shape[1]
    grid = vis.reshape(half, 2, half, 2, width).transpose(0, 2, 1, 3, 4)
    return grid.reshape(half * half, 4 * width)


def shift(size, step):
    return [(i, (i + step) % size) for i in range(size)]


def far_shift(size):
    return [(i, (i + (2 if i % 2 == 0 else -2)) % size) for i in range(size)]


def back_again(pairs):
    return [(b, a) for a, b in pairs]


def slot_tables(info, ids):
    tiles = info.shape[0]
    hit = info[:, :TOPK, None, :].astype(jnp.int32) == ids[None, None, :, None]
    member = jnp.any(hit, axis=1)
    weight = jnp.sum(jnp.where(hit, info[:, TOPK : 2 * TOPK, None, :], 0.0), axis=1)
    earlier = jnp.triu(jnp.ones((TPAD, TPAD), jnp.bfloat16), 1)
    before = jnp.dot(
        member.astype(jnp.bfloat16), earlier, preferred_element_type=jnp.float32
    ).astype(jnp.int32)
    place = jnp.where(member, before, -1)
    table = place[:, :, None, :] == jnp.arange(SLOT, dtype=jnp.int32)[None, None, :, None]
    high = weight.astype(jnp.bfloat16)
    low = (weight - high.astype(jnp.float32)).astype(jnp.bfloat16)
    zero = jnp.zeros((), jnp.bfloat16)
    shape = (tiles, ids.shape[0] * SLOT, TPAD)
    parts = [
        jnp.where(table, part[:, :, None, :], zero).reshape(shape).swapaxes(1, 2)
        for part in (high, low)
    ]
    return table.astype(jnp.bfloat16).reshape(shape), jnp.concatenate(parts, axis=1)


def merge_body(merged_ref, weight_ref, stream_ref):
    half = weight_ref.shape[2]
    dims = (((1,), (1,)), ((), ()))
    product = lax.dot_general(
        merged_ref[:, :half], weight_ref[0], dims, preferred_element_type=jnp.float32
    ) + lax.dot_general(
        merged_ref[:, half:], weight_ref[1], dims, preferred_element_type=jnp.float32
    )
    gelu = 0.5 * product * (1.0 + lax.erf(product * (0.5**0.5)))
    stream_ref[...] = gelu.astype(jnp.bfloat16)


def merge(merged, weight):
    width = weight.shape[1]
    block = 256
    return pl.pallas_call(
        merge_body,
        grid=(width // block,),
        in_specs=[
            pl.BlockSpec(merged.shape, lambda i: (0, 0)),
            pl.BlockSpec((2, block, weight.shape[2]), lambda i: (0, i, 0)),
        ],
        out_specs=pl.BlockSpec((TPAD, block), lambda i: (0, i)),
        out_shape=jax.ShapeDtypeStruct((TPAD, width), jnp.bfloat16),
        compiler_params=pltpu.CompilerParams(vmem_limit_bytes=60 << 20),
        cost_estimate=pl.CostEstimate(
            flops=2 * TPAD * width * merged.shape[1],
            bytes_accessed=7 << 20,
            transcendentals=TPAD * width,
        ),
        name="merge",
    )(merged, weight)


def pick_body(index, table_ref, tile_ref, *refs):
    send, rows, sem = refs[-3:]
    picked = jnp.dot(table_ref[0], tile_ref[...], preferred_element_type=jnp.float32)
    rows[...] = picked.astype(jnp.bfloat16).reshape(rows.shape)
    copy = pltpu.make_async_copy(rows, send.at[:, :, index], sem)
    copy.start()
    copy.wait()


def pick_rows(table, index, tile, shape, send=None):
    cols, hosted, _, slot, width = shape
    given = [] if send is None else [send]
    return pl.pallas_call(
        functools.partial(pick_body, index),
        grid=(1,),
        in_specs=[
            pl.BlockSpec((1,) + table.shape[1:], lambda i: (index, 0, 0)),
            pl.BlockSpec(tile.shape, lambda i: (0, 0)),
        ]
        + [pl.BlockSpec(memory_space=pltpu.HBM)] * len(given),
        out_specs=pl.BlockSpec(memory_space=pltpu.HBM),
        out_shape=jax.ShapeDtypeStruct(shape, jnp.bfloat16),
        scratch_shapes=[
            pltpu.VMEM((cols, hosted, slot, width), jnp.bfloat16),
            pltpu.SemaphoreType.DMA,
        ],
        input_output_aliases={2: 0} if given else {},
        compiler_params=pltpu.CompilerParams(vmem_limit_bytes=24 << 20),
        cost_estimate=pl.CostEstimate(
            flops=2 * TPAD * width * table.shape[1],
            bytes_accessed=1 << 20,
            transcendentals=0,
        ),
        name="pick_rows",
    )(table, tile, *given)


def expert_body(hidden, rows_hbm, gain_ref, weight_hbm, out_hbm, rows, weight, out, sems):
    cols, hosted, count, width = rows_hbm.shape
    span = weight_hbm.shape[1] // hosted
    first = 2 * hidden

    def load(j):
        copies = [
            pltpu.make_async_copy(rows_hbm.at[:, j], rows.at[j], sems.at[j, 0]),
            pltpu.make_async_copy(
                weight_hbm.at[:, pl.ds(j * span, first)],
                weight.at[j, :, pl.ds(0, first)],
                sems.at[j, 1],
            ),
            pltpu.make_async_copy(
                weight_hbm.at[:, pl.ds(j * span + first, span - first)],
                weight.at[j, :, pl.ds(first, span - first)],
                sems.at[j, 2],
            ),
        ]
        for copy in copies:
            copy.start()
        return copies

    pending = load(0)
    results = []
    for j in range(hosted):
        current = pending
        for copy in current:
            copy.wait()
        if j + 1 < hosted:
            pending = load(j + 1)
        for i in range(0, cols, 2):
            wide = rows[j, i : i + 2].reshape(-1, width).astype(jnp.float32)
            scale = lax.rsqrt(jnp.mean(wide * wide, axis=-1, keepdims=True) + 1e-06)
            normed = (wide * scale * gain_ref[...]).astype(jnp.bfloat16)
            both = jnp.dot(normed, weight[j, :, :first], preferred_element_type=jnp.float32)
            gate = both[:, :hidden]
            up = both[:, hidden:]
            act = (gate / (1.0 + jnp.exp(-gate)) * up).astype(jnp.bfloat16)
            out[j, i : i + 2] = (
                lax.dot_general(
                    act,
                    weight[j, :, first : first + hidden],
                    (((1,), (1,)), ((), ())),
                    preferred_element_type=jnp.float32,
                )
                .astype(jnp.bfloat16)
                .reshape(2, count, width)
            )
        result = pltpu.make_async_copy(out.at[j], out_hbm.at[:, j], sems.at[j, 3])
        result.start()
        results.append(result)
    for result in results:
        result.wait()


def expert_ffn(rows, gain, weight, hidden):
    cols, hosted, count, width = rows.shape
    held = (hosted, cols, count, width)
    hbm = pl.BlockSpec(memory_space=pltpu.HBM)
    return pl.pallas_call(
        functools.partial(expert_body, hidden),
        in_specs=[hbm, pl.BlockSpec(memory_space=pltpu.VMEM), hbm],
        out_specs=hbm,
        out_shape=jax.ShapeDtypeStruct(rows.shape, jnp.bfloat16),
        scratch_shapes=[
            pltpu.VMEM(held, jnp.bfloat16),
            pltpu.VMEM((hosted, width, weight.shape[1] // hosted), jnp.bfloat16),
            pltpu.VMEM(held, jnp.bfloat16),
            pltpu.SemaphoreType.DMA((hosted, 4)),
        ],
        compiler_params=pltpu.CompilerParams(vmem_limit_bytes=60 << 20),
        cost_estimate=pl.CostEstimate(
            flops=6 * cols * hosted * count * width * hidden,
            bytes_accessed=16 << 20,
            transcendentals=cols * hosted * count * hidden,
        ),
        name="expert_ffn",
    )(rows, gain, weight)


def combine_body(mix_ref, back_ref, out_ref):
    back = back_ref[...].reshape(mix_ref.shape[2], out_ref.shape[1])
    both = jnp.dot(mix_ref[0], back, preferred_element_type=jnp.float32)
    out_ref[...] = (both[:TPAD] + both[TPAD:]).astype(out_ref.dtype)


def combine(mix, back, index, dtype):
    cols, hosted, _, slot, width = back.shape
    return pl.pallas_call(
        combine_body,
        grid=(1,),
        in_specs=[
            pl.BlockSpec((1,) + mix.shape[1:], lambda i: (index, 0, 0)),
            pl.BlockSpec((cols, hosted, 1, slot, width), lambda i: (0, 0, index, 0, 0)),
        ],
        out_specs=pl.BlockSpec((TPAD, width), lambda i: (0, 0)),
        out_shape=jax.ShapeDtypeStruct((TPAD, width), dtype),
        compiler_params=pltpu.CompilerParams(vmem_limit_bytes=24 << 20),
        cost_estimate=pl.CostEstimate(
            flops=4 * TPAD * width * mix.shape[2],
            bytes_accessed=1 << 20,
            transcendentals=0,
        ),
        name="combine",
    )(mix, back)


def local(
    queries,
    keys,
    values,
    resid,
    w_out,
    w_merge,
    rms_gain,
    w_gate,
    w_up,
    w_down,
    tile_count,
    routes,
    route_weight,
):
    tokens = routes.shape[0]
    hidden = w_gate.shape[2]
    rows = lax.axis_size("y")
    cols = lax.axis_size("x")
    row = lax.axis_index("y")
    position = row * cols + lax.axis_index("x")
    page = position // MAXT
    count = lax.dynamic_index_in_dim(tile_count[0], page, keepdims=False)
    live = position % MAXT < count

    half = w_merge.shape[0] // 2
    piece = lax.dynamic_slice_in_dim(w_merge.T, lax.axis_index("core") * half, half, 1)
    piece = lax.all_to_all(
        jnp.broadcast_to(piece[None], (cols,) + piece.shape), "x", split_axis=0, concat_axis=0
    )
    piece = piece.reshape(-1, half)
    queries, w_gate, w_up, w_down, routes, route_weight, piece = lax.optimization_barrier(
        (queries, w_gate, w_up, w_down, routes, route_weight, piece)
    )
    merger = lax.all_gather(piece, ("core", "y"), axis=0, tiled=True)
    merger = merger.reshape(2, -1, half)

    down = w_down[0].T
    blank = jnp.zeros((down.shape[0], -(-3 * hidden // 128) * 128 - 3 * hidden), down.dtype)
    own = jnp.concatenate([w_gate[0], w_up[0], down, blank], axis=1)
    other = lax.ppermute(own, "y", shift(rows, rows // 2))
    routing = jnp.concatenate(
        [
            jnp.pad(routes, ((0, TPAD - tokens), (0, 0)), constant_values=-1).astype(jnp.float32),
            jnp.pad(route_weight, ((0, TPAD - tokens), (0, 0))),
        ],
        axis=1,
    ).T
    steps = (shift(rows, 1), shift(rows, -1), far_shift(rows))
    info = jnp.stack([routing] + [lax.ppermute(routing, "y", step) for step in steps])
    hosted = jnp.stack([row, (row + rows // 2) % rows])
    ids = (hosted[None, :] * cols + jnp.arange(cols, dtype=jnp.int32)[:, None]).reshape(-1)
    table, mix = slot_tables(info, ids)

    vis = tile_attention(queries, keys, values, resid, w_out)
    merged = jnp.where(live, space_to_depth(vis), jnp.zeros((), jnp.bfloat16))
    merged = jnp.pad(merged, ((0, TPAD - tokens), (0, 0)))

    own, other, merged, table, mix = lax.optimization_barrier((own, other, merged, table, mix))
    mine = jnp.concatenate([own, other], axis=1)
    experts = lax.all_gather(mine, ("z", "core"), axis=0, tiled=True)
    stream = merge(merged, merger)
    width = stream.shape[1]
    shape = (cols, 2, 1 + len(steps), SLOT, width)
    arrived = [lax.ppermute(stream, "y", step) for step in steps]
    send = pick_rows(table, 0, stream, shape)
    for i, tile in enumerate(arrived):
        send = pick_rows(table, i + 1, tile, shape, send)
    flat = (cols, send.size // cols // width, width)
    received = lax.all_to_all(send.reshape(flat), "x", split_axis=0, concat_axis=0)
    outcome = expert_ffn(
        received.reshape(cols, 2, -1, width),
        rms_gain[None, :],
        experts,
        hidden,
    )
    back = lax.all_to_all(outcome.reshape(flat), "x", split_axis=0, concat_axis=0)
    back = back.reshape(shape)
    parts = [
        lax.ppermute(combine(mix, back, i + 1, jnp.bfloat16), "y", back_again(step))
        for i, step in enumerate(steps)
    ]
    total = combine(mix, back, 0, jnp.float32) + stream.astype(jnp.float32)
    for part in parts:
        total = total + part.astype(jnp.float32)
    return total[:tokens].astype(jnp.bfloat16)


def solution(mesh):
    inner = Mesh(mesh.devices.reshape(8, 2, 8, 4), ("z", "core", "y", "x"))
    pages = ("z", "core")
    expert = ("y", "x")
    rows = P(("z", "core", "y", "x"), None)
    return jax.shard_map(
        local,
        mesh=inner,
        in_specs=(
            rows,
            rows,
            rows,
            rows,
            P(),
            P(None, expert),
            P(),
            P(expert, pages, None),
            P(expert, pages, None),
            P(expert, None, pages),
            P(pages, None),
            rows,
            rows,
        ),
        out_specs=rows,
        check_vma=False,
    )
```

```python
import functools
import jax
import jax.numpy as jnp
from jax import lax
from jax.experimental import pallas as pl
from jax.experimental.pallas import tpu as pltpu
from jax.sharding import Mesh
from jax.sharding import PartitionSpec as P

HEADS = 8
TS = 22
EXPERTS = 32
TOPK = 6
MAXT = 4
SLOT = 32
TPAD = 128


def tile_attention(queries, keys, values, resid, w_out):
    patches = queries.shape[0]
    head_size = queries.shape[1] // HEADS
    q_heads = queries.reshape(patches, HEADS, head_size)
    k_heads = keys.reshape(patches, HEADS, head_size)
    v_heads = values.reshape(patches, HEADS, head_size)
    scores = jnp.einsum(
        "qhd,khd->hqk", q_heads, k_heads, preferred_element_type=jnp.float32
    ) * head_size ** (-0.5)
    top = jnp.max(scores, axis=-1, keepdims=True)
    weights = jnp.exp(scores - top)
    probs = (weights / jnp.sum(weights, axis=-1, keepdims=True)).astype(jnp.bfloat16)
    attended = jnp.einsum(
        "hqk,khd->qhd", probs, v_heads, preferred_element_type=jnp.float32
    ).astype(jnp.bfloat16)
    update = jnp.dot(attended.reshape(patches, -1), w_out, preferred_element_type=jnp.float32)
    return (resid.astype(jnp.float32) + update).astype(jnp.bfloat16)


def space_to_depth(vis):
    half = TS // 2
    width = vis.shape[1]
    grid = vis.reshape(half, 2, half, 2, width).transpose(0, 2, 1, 3, 4)
    return grid.reshape(half * half, 4 * width)


def shift(size, step):
    return [(i, (i + step) % size) for i in range(size)]


def far_shift(size):
    return [(i, (i + (2 if i % 2 == 0 else -2)) % size) for i in range(size)]


def back_again(pairs):
    return [(b, a) for a, b in pairs]


def slot_tables(info, ids):
    tiles = info.shape[0]
    hit = info[:, :TOPK, None, :].astype(jnp.int32) == ids[None, None, :, None]
    member = jnp.any(hit, axis=1)
    weight = jnp.sum(jnp.where(hit, info[:, TOPK : 2 * TOPK, None, :], 0.0), axis=1)
    earlier = jnp.triu(jnp.ones((TPAD, TPAD), jnp.bfloat16), 1)
    before = jnp.dot(
        member.astype(jnp.bfloat16), earlier, preferred_element_type=jnp.float32
    ).astype(jnp.int32)
    place = jnp.where(member, before, -1)
    table = place[:, :, None, :] == jnp.arange(SLOT, dtype=jnp.int32)[None, None, :, None]
    high = weight.astype(jnp.bfloat16)
    low = (weight - high.astype(jnp.float32)).astype(jnp.bfloat16)
    zero = jnp.zeros((), jnp.bfloat16)
    shape = (tiles, ids.shape[0] * SLOT, TPAD)
    parts = [
        jnp.where(table, part[:, :, None, :], zero).reshape(shape).swapaxes(1, 2)
        for part in (high, low)
    ]
    return table.astype(jnp.bfloat16).reshape(shape), jnp.concatenate(parts, axis=1)


def merge_body(merged_ref, weight_ref, stream_ref):
    half = weight_ref.shape[2]
    dims = (((1,), (1,)), ((), ()))
    product = lax.dot_general(
        merged_ref[:, :half], weight_ref[0], dims, preferred_element_type=jnp.float32
    ) + lax.dot_general(
        merged_ref[:, half:], weight_ref[1], dims, preferred_element_type=jnp.float32
    )
    gelu = 0.5 * product * (1.0 + lax.erf(product * (0.5**0.5)))
    stream_ref[...] = gelu.astype(jnp.bfloat16)


def merge(merged, weight):
    width = weight.shape[1]
    block = 256
    return pl.pallas_call(
        merge_body,
        grid=(width // block,),
        in_specs=[
            pl.BlockSpec(merged.shape, lambda i: (0, 0)),
            pl.BlockSpec((2, block, weight.shape[2]), lambda i: (0, i, 0)),
        ],
        out_specs=pl.BlockSpec((TPAD, block), lambda i: (0, i)),
        out_shape=jax.ShapeDtypeStruct((TPAD, width), jnp.bfloat16),
        compiler_params=pltpu.CompilerParams(vmem_limit_bytes=60 << 20),
        cost_estimate=pl.CostEstimate(
            flops=2 * TPAD * width * merged.shape[1],
            bytes_accessed=7 << 20,
            transcendentals=TPAD * width,
        ),
        name="merge",
    )(merged, weight)


def pick_body(index, table_ref, tile_ref, *refs):
    send, rows, sem = refs[-3:]
    picked = jnp.dot(table_ref[0], tile_ref[...], preferred_element_type=jnp.float32)
    rows[...] = picked.astype(jnp.bfloat16).reshape(rows.shape)
    copy = pltpu.make_async_copy(rows, send.at[:, :, index], sem)
    copy.start()
    copy.wait()


def pick_rows(table, index, tile, shape, send=None):
    cols, hosted, _, slot, width = shape
    given = [] if send is None else [send]
    return pl.pallas_call(
        functools.partial(pick_body, index),
        grid=(1,),
        in_specs=[
            pl.BlockSpec((1,) + table.shape[1:], lambda i: (index, 0, 0)),
            pl.BlockSpec(tile.shape, lambda i: (0, 0)),
        ]
        + [pl.BlockSpec(memory_space=pltpu.HBM)] * len(given),
        out_specs=pl.BlockSpec(memory_space=pltpu.HBM),
        out_shape=jax.ShapeDtypeStruct(shape, jnp.bfloat16),
        scratch_shapes=[
            pltpu.VMEM((cols, hosted, slot, width), jnp.bfloat16),
            pltpu.SemaphoreType.DMA,
        ],
        input_output_aliases={2: 0} if given else {},
        compiler_params=pltpu.CompilerParams(vmem_limit_bytes=24 << 20),
        cost_estimate=pl.CostEstimate(
            flops=2 * TPAD * width * table.shape[1],
            bytes_accessed=1 << 20,
            transcendentals=0,
        ),
        name="pick_rows",
    )(table, tile, *given)


def expert_body(hidden, rows, gain_ref, weight_hbm, out_hbm, weight, out, load_sems, store_sems):
    cols, hosted, count, width = rows.shape
    first = 2 * hidden
    downs = hosted * first
    cut = -(-(downs + hidden) // 128) * 128
    spans = ((0, first), (downs, cut)), ((first, downs), (cut, weight.shape[1]))

    def load(j, part):
        start, stop = spans[j][part]
        lanes = pl.ds(start, stop - start)
        copy = pltpu.make_async_copy(
            weight_hbm.at[:, lanes], weight.at[:, lanes], load_sems.at[j, part]
        )
        copy.start()
        return copy

    pending = [load(0, 0), load(0, 1)]
    stores = []
    for j in range(hosted):
        last = j + 1 == hosted
        chunks = range(0, cols, 2)
        current, acts = pending, []
        current[0].wait()
        pending = [] if last else [load(j + 1, 0)]
        for i in chunks:
            wide = rows[i : i + 2, j].reshape(-1, width).astype(jnp.float32)
            scale = lax.rsqrt(jnp.mean(wide * wide, axis=-1, keepdims=True) + 1e-06)
            normed = (wide * scale * gain_ref[...]).astype(jnp.bfloat16)
            both = jnp.dot(normed, weight[:, j * first : (j + 1) * first], preferred_element_type=jnp.float32)
            gate = both[:, :hidden]
            up = both[:, hidden:]
            acts.append((gate / (1.0 + jnp.exp(-gate)) * up).astype(jnp.bfloat16))
        current[1].wait()
        if not last:
            pending.append(load(j + 1, 1))
        lead = (downs + j * hidden) % 128
        start = downs + j * hidden - lead
        for i, act in zip(chunks, acts):
            if lead:
                blank = jnp.zeros((act.shape[0], lead), act.dtype)
                act = jnp.concatenate([blank, act], axis=1)
            out[j, i : i + 2] = (
                lax.dot_general(
                    act,
                    weight[:, start : start + lead + hidden],
                    (((1,), (1,)), ((), ())),
                    preferred_element_type=jnp.float32,
                )
                .astype(jnp.bfloat16)
                .reshape(2, count, width)
            )
            store = pltpu.make_async_copy(
                out.at[j, pl.ds(i, 2)], out_hbm.at[pl.ds(i, 2), j], store_sems.at[j, i // 2]
            )
            store.start()
            stores.append(store)
    for store in stores:
        store.wait()


def expert_ffn(rows, gain, weight, hidden):
    cols, hosted, count, width = rows.shape
    vmem = pl.BlockSpec(memory_space=pltpu.VMEM)
    hbm = pl.BlockSpec(memory_space=pltpu.HBM)
    return pl.pallas_call(
        functools.partial(expert_body, hidden),
        in_specs=[vmem, vmem, hbm],
        out_specs=hbm,
        out_shape=jax.ShapeDtypeStruct(rows.shape, jnp.bfloat16),
        scratch_shapes=[
            pltpu.VMEM(weight.shape, jnp.bfloat16),
            pltpu.VMEM((hosted, cols, count, width), jnp.bfloat16),
            pltpu.SemaphoreType.DMA((hosted, 2)),
            pltpu.SemaphoreType.DMA((hosted, cols // 2)),
        ],
        compiler_params=pltpu.CompilerParams(vmem_limit_bytes=40 << 20),
        cost_estimate=pl.CostEstimate(
            flops=6 * cols * hosted * count * width * hidden,
            bytes_accessed=16 << 20,
            transcendentals=cols * hosted * count * hidden,
        ),
        name="expert_ffn",
    )(rows, gain, weight)


def combine_body(mix_ref, back_ref, out_ref):
    back = back_ref[...].reshape(mix_ref.shape[2], out_ref.shape[1])
    both = jnp.dot(mix_ref[0], back, preferred_element_type=jnp.float32)
    out_ref[...] = (both[:TPAD] + both[TPAD:]).astype(out_ref.dtype)


def combine(mix, back, index, dtype):
    cols, hosted, _, slot, width = back.shape
    return pl.pallas_call(
        combine_body,
        grid=(1,),
        in_specs=[
            pl.BlockSpec((1,) + mix.shape[1:], lambda i: (index, 0, 0)),
            pl.BlockSpec((cols, hosted, 1, slot, width), lambda i: (0, 0, index, 0, 0)),
        ],
        out_specs=pl.BlockSpec((TPAD, width), lambda i: (0, 0)),
        out_shape=jax.ShapeDtypeStruct((TPAD, width), dtype),
        compiler_params=pltpu.CompilerParams(vmem_limit_bytes=24 << 20),
        cost_estimate=pl.CostEstimate(
            flops=4 * TPAD * width * mix.shape[2],
            bytes_accessed=1 << 20,
            transcendentals=0,
        ),
        name="combine",
    )(mix, back)


def local(
    queries,
    keys,
    values,
    resid,
    w_out,
    w_merge,
    rms_gain,
    w_gate,
    w_up,
    w_down,
    tile_count,
    routes,
    route_weight,
):
    tokens = routes.shape[0]
    hidden = w_gate.shape[2]
    rows = lax.axis_size("y")
    cols = lax.axis_size("x")
    row = lax.axis_index("y")
    position = row * cols + lax.axis_index("x")
    page = position // MAXT
    count = lax.dynamic_index_in_dim(tile_count[0], page, keepdims=False)
    live = position % MAXT < count

    half = w_merge.shape[0] // 2
    piece = lax.dynamic_slice_in_dim(w_merge.T, lax.axis_index("core") * half, half, 1)
    piece = lax.all_to_all(
        jnp.broadcast_to(piece[None], (cols,) + piece.shape), "x", split_axis=0, concat_axis=0
    )
    piece = piece.reshape(-1, half)
    queries, w_gate, w_up, w_down, routes, route_weight, piece = lax.optimization_barrier(
        (queries, w_gate, w_up, w_down, routes, route_weight, piece)
    )
    merger = lax.all_gather(piece, ("core", "y"), axis=0, tiled=True)
    merger = merger.reshape(2, -1, half)

    own = jnp.concatenate([w_gate[0], w_up[0], w_down[0].T], axis=1)
    other = lax.ppermute(own, "y", shift(rows, rows // 2))
    routing = jnp.concatenate(
        [
            jnp.pad(routes, ((0, TPAD - tokens), (0, 0)), constant_values=-1).astype(jnp.float32),
            jnp.pad(route_weight, ((0, TPAD - tokens), (0, 0))),
        ],
        axis=1,
    ).T
    steps = (shift(rows, 1), shift(rows, -1), far_shift(rows))
    info = jnp.stack([routing] + [lax.ppermute(routing, "y", step) for step in steps])
    hosted = jnp.stack([row, (row + rows // 2) % rows])
    ids = (hosted[None, :] * cols + jnp.arange(cols, dtype=jnp.int32)[:, None]).reshape(-1)
    table, mix = slot_tables(info, ids)

    vis = tile_attention(queries, keys, values, resid, w_out)
    merged = jnp.where(live, space_to_depth(vis), jnp.zeros((), jnp.bfloat16))
    merged = jnp.pad(merged, ((0, TPAD - tokens), (0, 0)))

    own, other, merged, table, mix = lax.optimization_barrier((own, other, merged, table, mix))
    first = 2 * hidden
    mine = jnp.concatenate(
        [own[:, :first], other[:, :first], own[:, first:], other[:, first:]], axis=1
    )
    experts = lax.all_gather(mine, ("z", "core"), axis=0, tiled=True)
    stream = merge(merged, merger)
    width = stream.shape[1]
    shape = (cols, 2, 1 + len(steps), SLOT, width)
    arrived = [lax.ppermute(stream, "y", step) for step in steps]
    send = pick_rows(table, 0, stream, shape)
    for i, tile in enumerate(arrived):
        send = pick_rows(table, i + 1, tile, shape, send)
    flat = (cols, send.size // cols // width, width)
    received = lax.all_to_all(send.reshape(flat), "x", split_axis=0, concat_axis=0)
    outcome = expert_ffn(
        received.reshape(cols, 2, -1, width),
        rms_gain[None, :],
        experts,
        hidden,
    )
    back = lax.all_to_all(outcome.reshape(flat), "x", split_axis=0, concat_axis=0)
    back = back.reshape(shape)
    parts = [
        lax.ppermute(combine(mix, back, i + 1, jnp.bfloat16), "y", back_again(step))
        for i, step in enumerate(steps)
    ]
    total = combine(mix, back, 0, jnp.float32) + stream.astype(jnp.float32)
    for part in parts:
        total = total + part.astype(jnp.float32)
    return total[:tokens].astype(jnp.bfloat16)


def solution(mesh):
    inner = Mesh(mesh.devices.reshape(8, 2, 8, 4), ("z", "core", "y", "x"))
    pages = ("z", "core")
    expert = ("y", "x")
    rows = P(("z", "core", "y", "x"), None)
    return jax.shard_map(
        local,
        mesh=inner,
        in_specs=(
            rows,
            rows,
            rows,
            rows,
            P(),
            P(None, expert),
            P(),
            P(expert, pages, None),
            P(expert, pages, None),
            P(expert, None, pages),
            P(pages, None),
            rows,
            rows,
        ),
        out_specs=rows,
        check_vma=False,
    )
```
